256 devices in a mesh: pre: 4 (over z_hi), grp: 4 (over y), dec: 16 (over x, z_lo, core).
Axes of the slice: x: 4, y: 4, z: 8 (z_hi: 4, z_lo: 2; z = z_hi * 2 + z_lo), core: 2. Of those that a mesh axis runs over, the one named last changes fastest.
Arguments:
- cache: bfloat16 [64, 16384, 576], P('grp', ('pre', 'dec')), may hold values from -300 to 300
- cache_len: int32 [64], P('grp'), may hold values from 1 to 16384
- new_latent: bfloat16 [32, 16384, 576], P('grp', ('pre', 'dec')), may hold values from -6 to 6
- prompt_len: int32 [32], replicated, may hold values from 1 to 16384
- dest: int32 [32, 2], replicated, may hold values from 0 to 15, as said below
- q_latent: bfloat16 [3, 64, 1536], P(None, 'grp'), may hold values from -6 to 6
- new_kv: bfloat16 [3, 64, 576], P(None, 'grp'), may hold values from -6 to 6
- w_uq: bfloat16 [1536, 24576], P(None, ('pre', 'dec')), may hold values from -0.15625 to 0.15625
- w_uk: bfloat16 [128, 128, 512], P(('pre', 'dec')), may hold values from -0.5 to 0.5
- w_uv: bfloat16 [128, 512, 128], P(('pre', 'dec')), may hold values from -3 to 3
- w_o: bfloat16 [16384, 7168], P(('pre', 'dec')), may hold values from -0.125 to 0.125
Outputs:
- attended: bfloat16 [3, 64, 7168], P(None, 'grp', ('pre', 'dec'))
The draws below stay inside these ranges and needn't reach their ends.
Inputs may be any that keep to these rules, and one draw needn't show every extreme that they name: dest[r,0] is a decode group and dest[r,1] a slot of it; no two requests name the same slot; requests 2k and 2k+1 go to different groups; of the 8 requests in each block of new_latent held by one index of grp, exactly 2 go to each group.
All inputs are finite; a program needn't handle non-finite values.
Results may differ from the reference program's by a relative error of at most 0.035.
The reference program's roundings to bfloat16 on the way count: a program that leaves them out, or rounds other values in their place, can miss the bound.
Values may be sent and summed in bfloat16 or wider, within the bound.
A program may use at most 128 MiB of HBM per device.

```python
import math
import jax
import jax.numpy as jnp
from jax import lax

D = 7168
H = 128
DN = 128
DR = 64
DL = 512
DV = 128
QL = 1536
ROWS_GRP = 16
STEPS = 3
KD = 576
B = 64
S = 16384
NEW = 32
N_GRP = 4


def draw_cache(key, part):
    key = jax.random.fold_in(key, 3)
    first = jax.random.fold_in(key, 0)
    values = jax.random.normal(first, (B, S, KD), jnp.float32)
    return values.astype(jnp.bfloat16)


def draw_lengths(key, count):
    first, second = jax.random.split(key)
    values = jax.random.randint(first, (count,), 1, S + 1)
    where_top = jax.random.randint(second, (), 0, count)
    return values.at[where_top].set(S).astype(jnp.int32)


def draw_cache_len(key, part):
    key = jax.random.fold_in(key, 5)
    return draw_lengths(key, B)


def draw_prompt_len(key, part):
    key = jax.random.fold_in(key, 7)
    return draw_lengths(key, NEW)


def draw_dest(key, part):
    key = jax.random.fold_in(key, 11)
    first, second, third = jax.random.split(key, 3)
    order_pre = jax.random.permutation(first, N_GRP).astype(jnp.int32)
    offset = jax.random.randint(second, (), 1, N_GRP)
    shifts = jnp.stack([order_pre, (order_pre + offset) % N_GRP], -1)
    block = jnp.arange(N_GRP, dtype=jnp.int32)[:, None, None]
    group = (block + shifts[None, :, :]) % N_GRP
    lane = jnp.arange(2, dtype=jnp.int32)[None, None, :]
    rank = 2 * block + lane + 0 * group
    orders = jax.vmap(lambda k: jax.random.permutation(k, ROWS_GRP))(jax.random.split(third, N_GRP)).astype(jnp.int32)
    spots = jnp.arange(ROWS_GRP, dtype=jnp.int32)[None, :]
    head = orders[:, :1]
    orders = jnp.where(orders == ROWS_GRP - 1, head, jnp.where(spots == 0, ROWS_GRP - 1, orders))
    slot = orders[group, rank]
    return jnp.stack([group.reshape(-1), slot.reshape(-1)], -1).astype(jnp.int32)


def raised(result, own_key, source, target, shards_of, factor):
    def block_of(position):
        return (jnp.arange(result.shape[position]) // (result.shape[position] // shards_of)).reshape((-1,) + (1,) * (result.ndim - 1 - position))

    first = jax.random.permutation(own_key, shards_of)[block_of(target)]
    far = (block_of(target) + shards_of // 2) % shards_of
    return jnp.where((block_of(source) == first) | (block_of(source) == far), factor * result, result)


def shard_levels(own_key, extent, cuts, least, largest):
    gain = 1.0
    for dim, blocks in cuts:
        heights = jax.random.uniform(jax.random.fold_in(jax.random.fold_in(own_key, 6), dim), (blocks,), jnp.float32, least / len(cuts), largest / len(cuts))
        gain = gain * jnp.repeat(jnp.exp(heights), extent[dim] // blocks).reshape((-1,) + (1,) * (len(extent) - 1 - dim))
    return gain


def bell_draw(rng, shape, scale, reach, cuts=(), held_as=jnp.bfloat16):
    drawn = scale * jax.random.normal(rng, shape, jnp.float32)
    if cuts:
        drawn = drawn * shard_levels(rng, shape, cuts, -0.22, 0.18)
    return jnp.clip(drawn, -reach, reach).astype(held_as)


def heavy_noise(own_key, extent, spread, most, pieces, heavy, held_as=jnp.bfloat16):
    values = spread * jax.random.normal(own_key, extent, jnp.float32)
    if pieces:
        values = values * shard_levels(own_key, extent, pieces, -0.22, 0.18)
    return jnp.clip(raised(values, jax.random.fold_in(own_key, 3), *heavy), -most, most).astype(held_as)


def setup_inputs(seed: int = 0) -> dict:
    streams_of = jax.random.split(jax.random.key(seed), 12)
    return {
        "cache": draw_cache(jax.random.fold_in(streams_of[11], 71), 0),
        "cache_len": draw_cache_len(jax.random.fold_in(streams_of[11], 71), 0),
        "new_latent": bell_draw(streams_of[2], (NEW, S, KD), 1.0, 6.0, ((0, 4), (1, 64))),
        "prompt_len": draw_prompt_len(jax.random.fold_in(streams_of[11], 71), 0),
        "dest": draw_dest(jax.random.fold_in(streams_of[11], 71), 0),
        "q_latent": bell_draw(streams_of[5], (STEPS, B, QL), 1.0, 6.0, ((1, 4),)),
        "new_kv": bell_draw(streams_of[6], (STEPS, B, KD), 1.0, 6.0, ((1, 4),)),
        "w_uq": bell_draw(streams_of[7], (QL, H * (DN + DR)), QL ** -0.5, 0.15625, ((1, 64),)),
        "w_uk": bell_draw(streams_of[8], (H, DN, DL), DN ** -0.5, 0.5, ((0, 64),)),
        "w_uv": bell_draw(streams_of[9], (H, DL, DV), (max(DL // 128, 1)) ** -0.5, 3.0, ((0, 64),)),
        "w_o": heavy_noise(streams_of[10], (H * DV, D), (H * DV) ** -0.5, 0.125, ((0, 64),), (0, 1, 64, 4.0)),
    }


ROPE_BASE = 10000.0

def rotate(part, positions):
    half = part.shape[-1] // 2
    freq = ROPE_BASE ** (-jnp.arange(half, dtype=jnp.float32) / half)
    angle = positions.astype(jnp.float32)[:, :, None, None] * freq
    first = part[..., :half]
    second = part[..., half:]
    return jnp.concatenate([first * jnp.cos(angle) - second * jnp.sin(angle), first * jnp.sin(angle) + second * jnp.cos(angle)], -1)

def make_query(q_latent, w_uq, w_uk, positions):
    steps_n, rows_n, width = q_latent.shape
    heads = w_uk.shape[0]
    nope_dim = w_uk.shape[1]
    q_full = jnp.dot(q_latent.reshape(steps_n * rows_n, width), w_uq, preferred_element_type=jnp.float32)
    q_full = q_full.astype(jnp.bfloat16).reshape(steps_n, rows_n, heads, -1)
    absorbed = jnp.einsum('trhn,hnl->trhl', q_full[..., :nope_dim].astype(jnp.float32), w_uk.astype(jnp.float32)).astype(jnp.bfloat16)
    roped = rotate(q_full[..., nope_dim:].astype(jnp.float32), positions).astype(jnp.bfloat16)
    return jnp.concatenate([absorbed, roped], -1)

def reference(cache, cache_len, new_latent, prompt_len, dest, q_latent, new_kv, w_uq, w_uk, w_uv, w_o):
    scale = 1.0 / math.sqrt(DN + DR)
    rows = (dest[:, 0] * ROWS_GRP + dest[:, 1]).astype(jnp.int32)
    select = rows[:, None] == jnp.arange(B, dtype=jnp.int32)[None, :]
    hit = jnp.any(select, axis=0)
    source = lax.optimization_barrier(jnp.sum(jnp.where(select, jnp.arange(NEW, dtype=jnp.int32)[:, None], 0), axis=0)).astype(jnp.int32)
    lengths = jnp.where(hit, prompt_len[source], cache_len).astype(jnp.int32)
    positions = lengths[None, :] + jnp.arange(STEPS, dtype=jnp.int32)[:, None]
    query = make_query(q_latent, w_uq, w_uk, positions)

    def one_row(index):
        row_keys = jnp.where(hit[index], new_latent[source[index]], cache[index])
        keys = jnp.concatenate([row_keys, new_kv[:, index]], 0).astype(jnp.float32)
        q_row = query[:, index].astype(jnp.float32)
        scores = jnp.einsum('thk,sk->ths', q_row, keys) * scale
        place = jnp.arange(S + STEPS, dtype=jnp.int32)
        step_ids = jnp.arange(STEPS, dtype=jnp.int32)[:, None]
        valid = jnp.where(place[None, :] < S, place[None, :] < lengths[index], place[None, :] - S <= step_ids)
        valid = valid[:, None, :]
        masked = jnp.where(valid, scores, jnp.float32(-1e+30))
        top = lax.optimization_barrier(jnp.max(masked, axis=-1, keepdims=True))
        probs = jnp.where(valid, jnp.exp(masked - top), jnp.float32(0.0))
        total = lax.optimization_barrier(jnp.sum(probs, axis=-1, keepdims=True))
        rounded = lax.optimization_barrier(probs.astype(jnp.bfloat16))
        summed = jnp.einsum('ths,sl->thl', rounded.astype(jnp.float32), keys[:, :DL])
        return (summed / total).astype(jnp.bfloat16)
    latent_out = lax.map(one_row, jnp.arange(B, dtype=jnp.int32))
    latent_out = jnp.transpose(latent_out, (1, 0, 2, 3))
    head_out = jnp.einsum('tbhl,hlv->tbhv', latent_out.astype(jnp.float32), w_uv.astype(jnp.float32)).astype(jnp.bfloat16)
    flat = head_out.reshape(STEPS * B, H * DV)
    attended = jnp.dot(flat, w_o, preferred_element_type=jnp.float32).astype(jnp.bfloat16)
    return attended.reshape(STEPS, B, D)
```

```python
import functools
import math

import jax
import jax.numpy as jnp
from jax import lax
from jax.experimental import pallas as pl
from jax.experimental.pallas import tpu as pltpu
from jax.sharding import PartitionSpec as P

ROPE_BASE = 10000.0
MESH = pl.DeviceIdType.MESH
NEG = -1e30
BF = jnp.bfloat16
F32 = jnp.float32


def up(value, unit):
    return -(-value // unit) * unit


def dot(a, b, **kw):
    return jnp.dot(a, b, preferred_element_type=F32, **kw)


def dot_t(a, b):
    return lax.dot_general(a, b, (((1,), (1,)), ((), ())), preferred_element_type=F32)


def dot_c(a, b):
    return lax.dot_general(a, b, (((0,), (0,)), ((), ())), preferred_element_type=F32)


def onehot(rows, cols, source):
    i = lax.broadcasted_iota(jnp.int32, (rows, cols), 0)
    j = lax.broadcasted_iota(jnp.int32, (rows, cols), 1)
    return jnp.where(source(i) == j, 1.0, 0.0)


def kernel(
    dims,
    dest_ref, clen_ref, plen_ref, freq_ref, ql_ref, nkv_ref, wuq_ref, wuk_ref, wuv_ref,
    cache_ref, newl_ref, wo_ref,
    out_ref,
    cvm, nvm, wov, idx_v, idx, lens_v, sels, sely, pick,
    ysend, yrecv, kx, ko, qh, qsend, pq, ck, qg1, qg2, acc, rsr, st, rss, stm,
    sb, sst, rb, rst, lat, lo, fl, part, po, pr, xr, zs, zr, yos, yor,
    l_s, y_s, y_r, p_s, p_r, a1_s, a1_r, a2_s, a2_r, c_s, c_r, d_s, d_r,
    e_s, e_r, f_s, f_r, x_s, x_r, z_s, z_r, o_s, o_r,
):
    G, NX, NZ, NZL, T, R, HL, PERG, YP, KD, DL, DN, DR, QL, W, SLOTS = dims
    QC = T * 2 * HL
    CH = R * QC
    RT = R * T
    M = 2 * RT
    HM = up(RT, 16)
    RB = R // 2
    KP = up(KD, 128)
    NEW = G * R
    TS = T * SLOTS
    PT = PERG * T
    scale = 1.0 / math.sqrt(DN + DR)
    seq = cache_ref.shape[2]
    pre, grp, dec = lax.axis_index("pre"), lax.axis_index("grp"), lax.axis_index("dec")
    core = lax.rem(dec, 2)
    z = pre * NZL + lax.rem(dec // 2, NZL)
    x = dec // (2 * NZL)
    shard = pre * (2 * NZL * NX) + dec

    def at(xx, zz, cc, gg):
        return (zz // NZL, gg, xx * (2 * NZL) + lax.rem(zz, NZL) * 2 + cc)

    partner = at(x, z, 1 - core, grp)

    def x_peer(k):
        xx = lax.rem(x + k, NX)
        return xx, at(xx, z, core, grp)

    def z_peer(k):
        zz = lax.rem(z + k, NZ)
        return zz, at(x, zz, core, grp)

    def g_peer(k):
        gg = lax.rem(grp + k, G)
        return gg, at(x, z, core, gg)

    def copy(src, dst, s, r, dev):
        return pltpu.make_async_remote_copy(
            src_ref=src, dst_ref=dst, send_sem=s, recv_sem=r, device_id=dev, device_id_type=MESH
        )

    def rows(ref, start, count):
        return ref.at[pl.ds(pl.multiple_of(start, 16), count)]

    def iota(shape, axis):
        return lax.broadcasted_iota(jnp.int32, shape, axis)

    barrier = pltpu.get_barrier_semaphore()
    peers = [partner]
    peers += [x_peer(k)[1] for k in range(1, NX)]
    peers += [z_peer(k)[1] for k in range(1, NZ)]
    peers += [g_peer(k)[1] for k in range(1, G)]
    for dev in peers:
        pl.semaphore_signal(barrier, inc=1, device_id=dev, device_id_type=MESH)
    load_c = pltpu.make_async_copy(cache_ref, cvm, l_s.at[0])
    load_n = pltpu.make_async_copy(newl_ref, nvm, l_s.at[1])
    load_o = pltpu.make_async_copy(wo_ref, wov, l_s.at[2])
    load_c.start()

    to_row = dest_ref[0:1, :]
    spot_row = dest_ref[1:2, :]
    same = iota((NEW, NEW), 0) == iota((NEW, NEW), 1)
    to_col = jnp.sum(jnp.where(same, to_row, 0), axis=1, keepdims=True)
    spot_col = jnp.sum(jnp.where(same, spot_row, 0), axis=1, keepdims=True)
    here_row = to_row == grp
    hit = jnp.where((spot_row == iota((SLOTS, NEW), 0)) & here_row, 1, 0)
    left_col = 1 - jnp.sum(hit, axis=1, keepdims=True)

    def before(shape):
        slot = lax.rem(iota(shape, 1), SLOTS)
        return jnp.sum(jnp.where(iota(shape, 0) < slot, left_col, 0), axis=0, keepdims=True)

    def left(shape):
        slot = lax.rem(iota(shape, 1), SLOTS)
        return jnp.sum(jnp.where(iota(shape, 0) == slot, left_col, 0), axis=0, keepdims=True)

    before_t, left_t = before((SLOTS, TS)), left((SLOTS, TS))
    before_s, left_s = before((SLOTS, SLOTS)), left((SLOTS, SLOTS))
    is_surv = (before_s == iota((2 * R, SLOTS), 0)) & (left_s > 0) & (iota((2 * R, SLOTS), 0) < R)
    surv_col = jnp.sum(jnp.where(is_surv, iota((2 * R, SLOTS), 1), 0), axis=1, keepdims=True)
    idx_v[...] = jnp.broadcast_to(surv_col, idx_v.shape)
    fetch = pltpu.make_async_copy(idx_v, idx, l_s.at[3])
    fetch.start()
    row_of = iota((2 * R, NEW), 0) - R + grp * R
    is_mine = (iota((2 * R, NEW), 1) == row_of) & (iota((2 * R, NEW), 0) >= R)
    lens_col = jnp.sum(jnp.where(is_surv, clen_ref[...], 0), axis=1, keepdims=True) + jnp.sum(
        jnp.where(is_mine, plen_ref[...], 0), axis=1, keepdims=True
    )
    lens_v[...] = jnp.broadcast_to(lens_col, lens_v.shape)
    k_row, k_col = iota((NEW, NEW), 1), iota((NEW, NEW), 0)
    rank_row = jnp.sum(
        jnp.where((to_col == to_row) & (k_col // R == k_row // R) & (k_col < k_row), 1, 0),
        axis=0,
        keepdims=True,
    )
    i, j = iota((M, TS), 0), iota((M, TS), 1)
    sels[...] = jnp.where(
        (before_t == i // T) & (left_t > 0) & (j // SLOTS == i % T) & (i < RT), 1.0, 0.0
    ).astype(BF)
    i, j = iota((G * YP, NEW), 0), iota((G * YP, NEW), 1)
    u = i % YP
    from_k = jnp.where((j // R == i // YP) & here_row & (rank_row == u // T) & (u < PT), 1.0, 0.0)
    to_slot = jnp.where(spot_col == iota((NEW, TS), 1) % SLOTS, 1.0, 0.0)
    i, j = iota((G * YP, TS), 0), iota((G * YP, TS), 1)
    sely[...] = jnp.where(
        j // SLOTS == i % YP % T, dot(from_k.astype(BF), to_slot.astype(BF)), 0.0
    ).astype(BF)
    i, j = iota((M, NEW), 0), iota((M, NEW), 1)
    own_k = (j == (i - RT) // T + grp * R) & (i >= RT)
    key_col = jnp.sum(jnp.where(own_k, to_row * YP + rank_row * T, 0), axis=1, keepdims=True)
    i, j = iota((M, G * YP), 0), iota((M, G * YP), 1)
    pick[...] = jnp.where((key_col + i % T == j) & (i >= RT), 1.0, 0.0).astype(BF)
    ysend[:, :QL] = dot(sely[...], ql_ref[...]).astype(BF)
    ysend[:, QL : QL + KD] = dot(sely[...], nkv_ref[...]).astype(BF)

    pl.semaphore_wait(barrier, len(peers))
    done = []
    for k in range(1, G):
        gg, dev = g_peer(k)
        c = copy(rows(ysend, gg * YP, YP), rows(yrecv, grp * YP, YP), y_s.at[k], y_r.at[grp], dev)
        c.start()
        done.append(c)
    own = pl.ds(pl.multiple_of(grp * YP, 16), YP)
    yrecv[own, :] = ysend[own, :]

    keys = copy(kx, ko, p_s.at[0], p_r.at[0], partner)
    done.append(keys)

    @pl.when(core == 0)
    def _():
        copy(newl_ref, ko, p_s.at[0], p_r.at[0], partner).start()

    fetch.wait()
    load_c.wait()

    @pl.when(core == 1)
    def _():
        for j in range(R):
            kx[j] = cvm[idx[j, 0]]
        keys.start()
        load_n.start()

    load_o.start()

    half_dr = DR // 2
    lens_row = jnp.sum(
        jnp.where(iota((2 * R, 2 * R), 0) == iota((2 * R, 2 * R), 1), lens_col, 0),
        axis=0,
        keepdims=True,
    )

    def produce(half):
        i = iota((HM, 2 * R), 0)
        found = jnp.where((iota((HM, 2 * R), 1) == half * R + i // T) & (i < RT), lens_row, 0)
        pos = jnp.sum(found, axis=1, keepdims=True) + iota((HM, 1), 0) % T
        angle = pos.astype(F32) * freq_ref[...]
        cos, sin = jnp.cos(angle), jnp.sin(angle)
        sin = jnp.where(iota((HM, DR), 1) < half_dr, -sin, sin)
        if half == 0:
            xin = dot(sels[:HM, :], ql_ref[...]).astype(BF)
        else:
            i = iota((HM, M), 0)
            low = jnp.where((iota((HM, M), 1) == i + RT) & (i < RT), 1.0, 0.0).astype(BF)
            xin = dot(dot(low, pick[...]).astype(BF), yrecv[:, :QL]).astype(BF)
        qf = dot(xin, wuq_ref[...]).astype(BF)
        HD = DN + DR
        for h in range(HL):
            nope = dot(qf, onehot(HL * HD, DN, lambda i: i - h * HD).astype(BF)).astype(BF)
            qh[h, :, :DL] = dot(nope, wuk_ref[h]).astype(BF)
            turned = lambda i: jnp.where(
                (i >= h * HD + DN) & (i < (h + 1) * HD), (i - h * HD - DN + half_dr) % DR, -1
            )
            rot = dot(qf, onehot(HL * HD, DR, lambda i: i - h * HD - DN).astype(BF))
            swp = dot(qf, onehot(HL * HD, DR, turned).astype(BF))
            qh[h, :, DL:] = (rot * cos + swp * sin).astype(BF)
        total = None
        for h in range(HL):
            sel = onehot(
                HL * RT,
                HM,
                lambda i: jnp.where((i >= h * RT) & (i < (h + 1) * RT), i - h * RT, -1),
            ).astype(BF)
            term = dot(sel, qh[h])
            total = term if total is None else total + term
        return total.astype(BF)

    def incoming():
        for k in range(1, G):
            gg, dev = g_peer(k)
            copy(
                rows(ysend, gg * YP, YP), rows(yrecv, gg * YP, YP), y_s.at[k], y_r.at[gg], dev
            ).wait_recv()

    def to_partner(block):
        qsend[...] = block
        c = copy(qsend, pq.at[core], p_s.at[1], p_r.at[1], partner)
        c.start()

    def gather_chunk():
        copy(qsend, pq.at[1 - core], p_s.at[1], p_r.at[1], partner).wait_recv()
        regroup = onehot(
            CH, CH, lambda i: i % (2 * HL) * RT + i // QC * T + i % QC // (2 * HL)
        ).astype(BF)
        ck[...] = (dot(regroup, pq[...].reshape(CH, KD))).astype(BF)

    done.append(copy(qsend, pq.at[core], p_s.at[1], p_r.at[1], partner))

    def spread(cc, n1, i1, peer1, n2, i2, peer2):
        w = n1 * QC
        blk = R * w
        sub = RB * w
        sends = []

        def hops(n, b, d):
            return n // 2 if (b == 0) == (d == 0) else n - 1 - n // 2

        def ring(n, i, d, k):
            return lax.rem(i + (k if d == 0 else n - k), n)

        def forward(n, i, peer, ref, blk, sub, s_sem, r_sem, b, h):
            for d in range(2):
                if h > hops(n, b, d):
                    continue
                _, dev = peer(1 if d == 0 else n - 1)
                origin = ring(n, i, 1 - d, h - 1)
                here = rows(ref, origin * blk + b * sub, sub)
                c = copy(here, here, s_sem.at[b, d, h], r_sem.at[b, origin], dev)
                if h > 1:
                    c.wait_recv()
                c.start()
                sends.append(c)

        def settle(n, i, peer, ref, blk, sub, s_sem, r_sem, b):
            for k in range(1, n):
                j, dev = peer(k)
                d = 1 if k <= hops(n, b, 1) else 0
                if (k if d == 1 else n - k) < hops(n, b, d):
                    continue
                here = rows(ref, j * blk + b * sub, sub)
                copy(here, here, s_sem.at[b, 0, 1], r_sem.at[b, j], dev).wait_recv()

        first = (n1, i1, peer1, qg1, CH, CH // 2, a1_s, a1_r)
        second = (n2, i2, peer2, qg2, blk, sub, a2_s, a2_r)
        if cc == 0:
            pq[0] = produce(0)
        else:
            to_partner(produce(0))
            incoming()
            pq[1] = produce(1)
        gather_chunk()
        qg1[pl.ds(pl.multiple_of(i1 * CH, 16), CH), :] = ck[...]
        for b in range(2):
            forward(*first, b, 1)
        if cc == 0:
            incoming()
            to_partner(produce(1))
        for h in range(2, n1 // 2 + 1):
            for b in range(2):
                forward(*first, b, h)

        def pack(b):
            part_rows = CH // 2
            source = jnp.concatenate(
                [qg1[pl.ds(o * CH + b * part_rows, part_rows), :] for o in range(n1)], 0
            )

            def one(r, _):
                sel = onehot(
                    w, n1 * part_rows, lambda i: i // QC * part_rows + r * QC + i % QC
                ).astype(BF)
                here = pl.ds(pl.multiple_of(i2 * blk + b * sub + r * w, 16), w)
                qg2[here, :] = dot(sel, source).astype(BF)
                return 0

            lax.fori_loop(0, RB, one, 0)

        for b in range(2):
            settle(*first, b)
            pack(b)
            forward(*second, b, 1)
        for h in range(2, n2 // 2 + 1):
            for b in range(2):
                forward(*second, b, h)
        big = n2 // 2
        copy(kx, ko, p_s.at[0], p_r.at[0], partner).wait_recv()
        if cc == 1:
            load_n.wait()

        st[...] = jnp.full(st.shape, NEG, F32)
        nq = n2 * w

        def attend(r, _):
            q = jnp.concatenate(
                [qg2[pl.ds(pl.multiple_of(o * blk + r * w, 16), w), :] for o in range(n2)], 0
            )
            if cc == 0:
                k_a, k_b = cvm[idx[r, 0]], ko[r]
            else:
                k_a, k_b = ko[r], nvm[r]
            mine = jnp.where(iota(lens_v.shape, 0) == r + cc * R, lens_v[...], 0)
            length = jnp.sum(mine, axis=0, keepdims=True)[:, :1]
            base = (shard - core) * seq
            place = base + lax.broadcasted_iota(jnp.int32, (nq, seq), 1)
            ok_a, ok_b = place < length, place + seq < length
            s_a = jnp.where(ok_a, dot(q, k_a) * scale, NEG)
            s_b = jnp.where(ok_b, dot(q, k_b) * scale, NEG)
            top = jnp.maximum(
                jnp.max(s_a, axis=1, keepdims=True), jnp.max(s_b, axis=1, keepdims=True)
            )
            p_a = jnp.where(ok_a, jnp.exp(s_a - top), 0.0)
            p_b = jnp.where(ok_b, jnp.exp(s_b - top), 0.0)
            total = jnp.sum(p_a, axis=1, keepdims=True) + jnp.sum(p_b, axis=1, keepdims=True)
            summed = dot_t(p_a.astype(BF), k_a[:DL, :]) + dot_t(p_b.astype(BF), k_b[:DL, :])
            some = total > 0.0
            safe = jnp.where(some, total, 1.0)
            value = (summed * (1.0 / safe)).astype(BF)
            lse = jnp.where(some, top + jnp.log(safe), NEG)
            for o in range(n2):
                acc[pl.ds(pl.multiple_of(o * blk + r * w, 16), w), :] = value[o * w : (o + 1) * w]
            b = r // RB
            lane = lax.broadcasted_iota(jnp.int32, (nq, 128), 1)
            st[b] = jnp.where(lane == r, lse, st[b])
            return 0

        def slot(b, d, h):
            return b * (n2 - 1) + (0 if d == 0 else hops(n2, b, 0)) + h - 1

        def merge(b, target, slots):
            here = pl.ds(pl.multiple_of(target * w, 16), w)
            parts = [st[b, here, :]] + [rss[s * w : (s + 1) * w, :] for s in slots]
            top = functools.reduce(jnp.maximum, parts)
            weights = [jnp.exp(p - top) for p in parts]
            total = functools.reduce(jnp.add, weights)
            weights = [v / total for v in weights]
            st[b, here, :] = top + jnp.log(total)
            lane = lax.broadcasted_iota(jnp.int32, (w, 128), 1)

            def one(r, _):
                mine = pl.ds(pl.multiple_of(target * blk + b * sub + r * w, 16), w)
                values = [acc[mine, :]]
                for s in slots:
                    values.append(rsr[pl.ds(pl.multiple_of(s * sub + r * w, 16), w), :])
                out = None
                for v, g in zip(values, weights):
                    col = jnp.sum(jnp.where(lane == b * RB + r, g, 0.0), axis=1, keepdims=True)
                    term = v.astype(F32) * col
                    out = term if out is None else out + term
                acc[mine, :] = out.astype(BF)
                return 0

            lax.fori_loop(0, RB, one, 0)

        def reduce_copies(b, d, h, target, dev):
            s = slot(b, d, h)
            big_copy = copy(
                rows(acc, target * blk + b * sub, sub),
                rsr.at[pl.ds(s * sub, sub)],
                c_s.at[b, d, h],
                c_r.at[b, d, h],
                dev,
            )
            small_copy = copy(
                st.at[b, pl.ds(pl.multiple_of(target * w, 16), w)],
                rss.at[pl.ds(s * w, w)],
                d_s.at[b, d, h],
                d_r.at[b, d, h],
                dev,
            )
            return big_copy, small_copy

        def step(b, d, h):
            if h > hops(n2, b, d):
                return
            _, dev = peer2(1 if d == 0 else n2 - 1)
            target = ring(n2, i2, d, hops(n2, b, d) - h + 1)
            if h > 1:
                for c in reduce_copies(b, d, h - 1, target, dev):
                    c.wait_recv()
                merge(b, target, [slot(b, d, h - 1)])
            for c in reduce_copies(b, d, h, target, dev):
                c.start()
                sends.append(c)

        for b in range(2):
            settle(*second, b)
            lax.fori_loop(b * RB, (b + 1) * RB, attend, 0)
            for d in range(2):
                step(b, d, 1)
        for h in range(2, big + 1):
            for b in range(2):
                for d in range(2):
                    step(b, d, h)
        for b in range(2):
            slots = []
            for d in range(2):
                last = hops(n2, b, d)
                if last:
                    _, dev = peer2(1 if d == 0 else n2 - 1)
                    for c in reduce_copies(b, d, last, i2, dev):
                        c.wait_recv()
                    slots.append(slot(b, d, last))
            if slots:
                merge(b, i2, slots)

        here = pl.ds(pl.multiple_of(i2 * w, 16), w)
        lane = lax.broadcasted_iota(jnp.int32, (w, 128), 1)
        stm[:w, :] = jnp.where(lane < RB, st[0, here, :], st[1, here, :])
        block = pl.ds(pl.multiple_of(i2 * blk, 16), blk)
        for k in range(1, n1 + 1):
            j, dev = peer1(k)
            sel = onehot(CH, blk, lambda i: i // QC * w + j * QC + i % QC).astype(BF)
            value = dot(sel, acc[block, :]).astype(BF)
            sel = onehot(16, w, lambda i: jnp.where(i < QC, j * QC + i, -1))
            stat = dot(sel, stm[:w, :], precision=lax.Precision.HIGHEST)
            if k == n1:
                rb[pl.ds(pl.multiple_of(i1 * CH, 16), CH), :] = value
                rst[pl.ds(pl.multiple_of(i1 * 16, 16), 16), :] = stat
            else:
                sb[k] = value
                sst[k] = stat
                for c in (
                    copy(sb.at[k], rows(rb, i1 * CH, CH), e_s.at[k], e_r.at[i1], dev),
                    copy(sst.at[k], rows(rst, i1 * 16, 16), f_s.at[k], f_r.at[i1], dev),
                ):
                    c.start()
                    sends.append(c)
        for k in range(1, n1):
            j, dev = peer1(k)
            copy(sb.at[k], rows(rb, j * CH, CH), e_s.at[k], e_r.at[j], dev).wait_recv()
            copy(sst.at[k], rows(rst, j * 16, 16), f_s.at[k], f_r.at[j], dev).wait_recv()

        if cc == 0:
            nkv = dot(sels[...], nkv_ref[...]).astype(BF)
        else:
            mine = onehot(M, M, lambda i: jnp.where(i < RT, i + RT, -1)).astype(BF)
            mine = dot(mine, pick[...]).astype(BF)
            nkv = dot(mine, yrecv[:, QL : QL + KD]).astype(BF)
        fresh = dot_t(ck[...], nkv) * scale
        i = lax.broadcasted_iota(jnp.int32, (CH, M), 0)
        j = lax.broadcasted_iota(jnp.int32, (CH, M), 1)
        seen = (i // QC == j // T) & (j % T <= i % QC // (2 * HL)) & (j < RT)
        fresh = jnp.where(seen, fresh, NEG)
        fill = onehot(CH, 16, lambda i: i % QC)
        own_row = lax.broadcasted_iota(jnp.int32, (CH, 128), 0) // QC
        lane = lax.broadcasted_iota(jnp.int32, (CH, 128), 1)
        lses = []
        for s in range(n1):
            spread_out = dot(fill, rst[s * 16 : (s + 1) * 16, :], precision=lax.Precision.HIGHEST)
            lses.append(
                jnp.sum(jnp.where(lane == own_row, spread_out, 0.0), axis=1, keepdims=True)
            )
        top = functools.reduce(jnp.maximum, lses, jnp.max(fresh, axis=1, keepdims=True))
        probs = jnp.where(seen, jnp.exp(fresh - top), 0.0)
        total = jnp.sum(probs, axis=1, keepdims=True)
        summed = dot(probs.astype(BF), nkv[:, :DL])
        for s in range(n1):
            g = jnp.exp(lses[s] - top)
            total = total + g
            summed = summed + rb[s * CH : (s + 1) * CH, :].astype(F32) * g
        lat[...] = (summed / total).astype(BF)
        for c in sends:
            c.wait_send()

    @pl.when(core == 0)
    def _():
        spread(0, NX, x, x_peer, NZ, z, z_peer)

    @pl.when(core == 1)
    def _():
        spread(1, NZ, z, z_peer, NX, x, x_peer)

    def heads_of(cc):
        sel = onehot(
            HL * RT,
            CH,
            lambda i: i % RT // T * QC + i % T * (2 * HL) + cc * HL + i // RT,
        ).astype(BF)
        return dot(sel, lat[...]).astype(BF)

    fl[...] = heads_of(1 - core)
    swap = copy(fl, lo.at[core], p_s.at[2], p_r.at[2], partner)
    swap.start()
    done.append(swap)
    lo[core] = heads_of(core)
    copy(fl, lo.at[1 - core], p_s.at[2], p_r.at[2], partner).wait_recv()
    every = lo[...].reshape(2 * HL * RT, DL)
    flat = []
    for h in range(HL):
        value = dot(every, wuv_ref[h]).astype(BF)
        sel = onehot(M, 2 * HL * RT, lambda i: i // RT * (HL * RT) + h * RT + i % RT).astype(BF)
        flat.append(dot(sel, value).astype(BF))
    flat = jnp.concatenate(flat, 1)
    load_o.wait()
    part[...] = dot(flat, wov[...])
    shards = 2 * NX * NZ
    for s in range(shards):
        s_pre, rest = divmod(s, 2 * NZL * NX)
        s_x, rest = divmod(rest, 2 * NZL)
        s_zl, s_core = divmod(rest, 2)
        first = s * W // 128
        off = s * W - first * 128
        if off + W <= 128:
            piece = part[:, first * 128 : (first + 1) * 128]
            if off:
                piece = pltpu.roll(piece, 128 - off, 1)
        else:
            piece = pltpu.roll(part[:, first * 128 : (first + 2) * 128], 256 - off, 1)[:, :128]
        po[s_core, s_x, s_pre * NZL + s_zl] = piece
    swap = copy(po.at[1 - core], pr, p_s.at[3], p_r.at[3], partner)
    swap.start()
    done.append(swap)
    swap.wait_recv()
    po[core] = po[core] + pr[...]
    halves = NZ // 2

    def x_hops(b, d):
        return NX // 2 if (b == 0) == (d == 0) else NX - 1 - NX // 2

    def x_slot(b, d, h):
        return b * (NX - 1) + (0 if d == 0 else x_hops(b, 0)) + h - 1

    def x_copy(b, d, h, target):
        _, dev = x_peer(1 if d == 0 else NX - 1)
        return copy(
            po.at[core, target, pl.ds(b * halves, halves)],
            xr.at[x_slot(b, d, h)],
            x_s.at[b, d, h],
            x_r.at[b, d, h],
            dev,
        )

    for h in range(1, NX // 2 + 1):
        for b in range(2):
            for d in range(2):
                if h > x_hops(b, d):
                    continue
                ahead = x_hops(b, d) - h + 1
                target = lax.rem(x + (ahead if d == 0 else NX - ahead), NX)
                if h > 1:
                    x_copy(b, d, h - 1, target).wait_recv()
                    span = pl.ds(b * halves, halves)
                    po[core, target, span] = po[core, target, span] + xr[x_slot(b, d, h - 1)]
                c = x_copy(b, d, h, target)
                c.start()
                done.append(c)
    for b in range(2):
        span = pl.ds(b * halves, halves)
        total = po[core, x, span]
        for d in range(2):
            last = x_hops(b, d)
            if last:
                x_copy(b, d, last, x).wait_recv()
                total = total + xr[x_slot(b, d, last)]
        zs[b * halves : (b + 1) * halves] = total
    for k in range(1, NZ):
        j, dev = z_peer(k)
        c = copy(zs.at[j], zr.at[z], z_s.at[k], z_r.at[z], dev)
        c.start()
        done.append(c)
    total = zs[z]
    for k in range(1, NZ):
        j, dev = z_peer(k)
        copy(zs.at[j], zr.at[j], z_s.at[k], z_r.at[j], dev).wait_recv()
        total = total + zr[j]
    final = total.astype(BF)
    yos[...] = dot_c(pick[...], final).astype(BF)
    for k in range(1, G):
        gg, dev = g_peer(k)
        c = copy(rows(yos, gg * YP, YP), rows(yor, grp * YP, YP), o_s.at[k], o_r.at[grp], dev)
        c.start()
        done.append(c)
    yor[own, :] = yos[own, :]
    for k in range(1, G):
        gg, dev = g_peer(k)
        copy(
            rows(yos, gg * YP, YP), rows(yor, gg * YP, YP), o_s.at[k], o_r.at[gg], dev
        ).wait_recv()
    placed = dot_c(sels[...], final) + dot_c(sely[...], yor[...])
    out_ref[...] = placed[:, :W].astype(BF)
    for c in done:
        c.wait_send()


def local(sizes, cache, cache_len, new_latent, prompt_len, dest, q_latent, new_kv, w_uq, w_uk, w_uv, w_o):
    G, NX, NZ, NZL = sizes
    rows_n, seq, KD = cache.shape
    T, _, QL = q_latent.shape
    HL, DN, DL = w_uk.shape
    DR = KD - DL
    R = new_latent.shape[0]
    PERG = R // G
    YP = up(PERG * T, 16)
    shards = 2 * NX * NZ
    W = w_o.shape[1] // shards
    M = 2 * R * T
    HM = up(R * T, 16)
    QC = T * 2 * HL
    CH = R * QC
    nq = NX * NZ * QC
    KP = up(KD, 128)
    half = DR // 2
    freq = ROPE_BASE ** (-jnp.arange(half, dtype=F32) / half)
    freq = jnp.concatenate([freq, freq])[None, :]
    dims = (G, NX, NZ, NZL, T, R, HL, PERG, YP, KD, DL, DN, DR, QL, W, rows_n)
    tall = max(NX, NZ)

    def slots_rows(n1, n2, per):
        return 2 * (n2 - 1) * n1 * QC * per

    rsr_rows = max(slots_rows(NX, NZ, R // 2), slots_rows(NZ, NX, R // 2), 16)
    rss_rows = max(slots_rows(NX, NZ, 1), slots_rows(NZ, NX, 1), 16)
    hop = tall // 2 + 1
    vmem = pl.BlockSpec(memory_space=pltpu.VMEM)
    anywhere = pl.BlockSpec(memory_space=pl.ANY)
    dma = pltpu.SemaphoreType.DMA
    V = pltpu.VMEM
    out = pl.pallas_call(
        functools.partial(kernel, dims),
        out_shape=jax.ShapeDtypeStruct((T * rows_n, W), BF),
        in_specs=[vmem] * 9 + [anywhere] * 3,
        out_specs=vmem,
        scratch_shapes=[
            V((rows_n, KD, seq), BF),
            V((R, KD, seq), BF),
            V(w_o.shape, BF),
            V((2 * R, 128), jnp.int32),
            pltpu.SMEM((2 * R, 128), jnp.int32),
            V((2 * R, 128), jnp.int32),
            V((M, T * rows_n), BF),
            V((G * YP, T * rows_n), BF),
            V((M, G * YP), BF),
            V((G * YP, QL + KP), BF),
            V((G * YP, QL + KP), BF),
            V((R, KD, seq), BF),
            V((R, KD, seq), BF),
            V((HL, HM, KD), BF),
            V((HL * R * T, KD), BF),
            V((2, HL * R * T, KD), BF),
            V((CH, KD), BF),
            V((tall * CH, KD), BF),
            V((R * nq, KD), BF),
            V((R * nq, DL), BF),
            V((rsr_rows, DL), BF),
            V((2, nq, 128), F32),
            V((rss_rows, 128), F32),
            V((tall * QC, 128), F32),
            V((tall, CH, DL), BF),
            V((tall, 16, 128), F32),
            V((tall * CH, DL), BF),
            V((tall * 16, 128), F32),
            V((CH, DL), BF),
            V((2, HL * R * T, DL), BF),
            V((HL * R * T, DL), BF),
            V((M, shards * W), F32),
            V((2, NX, NZ, M, 128), F32),
            V((NX, NZ, M, 128), F32),
            V((2 * max(NX - 1, 1), NZ // 2, M, 128), F32),
            V((NZ, M, 128), F32),
            V((NZ, M, 128), F32),
            V((G * YP, 128), BF),
            V((G * YP, 128), BF),
            dma((4,)), dma((G,)), dma((G,)), dma((4,)), dma((4,)),
            dma((2, 2, hop)), dma((2, tall)), dma((2, 2, hop)), dma((2, tall)),
            dma((2, 2, hop)), dma((2, 2, hop)), dma((2, 2, hop)), dma((2, 2, hop)),
            dma((tall,)), dma((tall,)), dma((tall,)), dma((tall,)),
            dma((2, 2, hop)), dma((2, 2, hop)), dma((NZ,)), dma((NZ,)), dma((G,)), dma((G,)),
        ],
        compiler_params=pltpu.CompilerParams(
            collective_id=0, has_side_effects=True, vmem_limit_bytes=60 * 2**20
        ),
    )(
        dest.T,
        cache_len[None, :],
        prompt_len[None, :],
        freq,
        q_latent.reshape(T * rows_n, QL),
        new_kv.reshape(T * rows_n, KD),
        w_uq,
        w_uk,
        w_uv,
        cache.transpose(0, 2, 1),
        new_latent.transpose(0, 2, 1),
        w_o,
    )
    return out.reshape(T, rows_n, W)


def solution(mesh):
    placed = (
        P("grp", ("pre", "dec"), None),
        P("grp"),
        P("grp", ("pre", "dec"), None),
        P(),
        P(),
        P(None, "grp", None),
        P(None, "grp", None),
        P(None, ("pre", "dec")),
        P(("pre", "dec"), None, None),
        P(("pre", "dec"), None, None),
        P(("pre", "dec"), None),
    )
    zl = 2
    sizes = (
        mesh.shape["grp"],
        mesh.shape["dec"] // (2 * zl),
        mesh.shape["pre"] * zl,
        zl,
    )
    return jax.shard_map(
        functools.partial(local, sizes),
        mesh=mesh,
        in_specs=placed,
        out_specs=P(None, "grp", ("pre", "dec")),
        check_vma=False,
    )
```

```python
import functools
import math

import jax
import jax.numpy as jnp
from jax import lax
from jax.experimental import pallas as pl
from jax.experimental.pallas import tpu as pltpu
from jax.sharding import PartitionSpec as P

ROPE_BASE = 10000.0
MESH = pl.DeviceIdType.MESH
NEG = -1e30
BF = jnp.bfloat16
F32 = jnp.float32


def up(value, unit):
    return -(-value // unit) * unit


def dot(a, b, **kw):
    return jnp.dot(a, b, preferred_element_type=F32, **kw)


def dot_t(a, b):
    return lax.dot_general(a, b, (((1,), (1,)), ((), ())), preferred_element_type=F32)


def dot_c(a, b):
    return lax.dot_general(a, b, (((0,), (0,)), ((), ())), preferred_element_type=F32)


def onehot(rows, cols, source):
    i = lax.broadcasted_iota(jnp.int32, (rows, cols), 0)
    j = lax.broadcasted_iota(jnp.int32, (rows, cols), 1)
    return jnp.where(source(i) == j, 1.0, 0.0)


def kernel(
    dims,
    dest_ref, clen_ref, plen_ref, freq_ref, ql_ref, nkv_ref, wuq_ref, wuk_ref, wuv_ref,
    cache_ref, newl_ref, wo_ref,
    out_ref,
    cvm, nvm, wov, idx_v, idx, lens_v, sels, sely, selh, pick, xlo, xhi,
    ysend, yrecv, kx, ko, qh, qsend, pq, ck, qall, qp, acc, rsr, st, rss,
    sb, sst, rb, rst, lat, lo, fl, part, po, pr, xs, xr, zs, zr, yos, yor,
    l_s, y_s, y_r, p_s, p_r, a1_s, a1_r, a2_s, a2_r, c_s, c_r, d_s, d_r,
    e_s, e_r, f_s, f_r, x_s, x_r, z_s, z_r, o_s, o_r,
):
    G, NX, NZ, NZL, T, R, HL, PERG, YP, KD, DL, DN, DR, QL, W, SLOTS, QA = dims
    QC = T * 2 * HL
    CH = R * QC
    RT = R * T
    M = 2 * RT
    HM = up(RT, 16)
    RB = R // 2
    RQ = R // 4
    QB = QL - QA
    NEW = G * R
    TS = T * SLOTS
    PT = PERG * T
    scale = 1.0 / math.sqrt(DN + DR)
    seq = cache_ref.shape[2]
    pre, grp, dec = lax.axis_index("pre"), lax.axis_index("grp"), lax.axis_index("dec")
    core = lax.rem(dec, 2)
    z = pre * NZL + lax.rem(dec // 2, NZL)
    x = dec // (2 * NZL)
    shard = pre * (2 * NZL * NX) + dec

    def at(xx, zz, cc, gg):
        return (zz // NZL, gg, xx * (2 * NZL) + lax.rem(zz, NZL) * 2 + cc)

    partner = at(x, z, 1 - core, grp)

    def x_peer(k):
        xx = lax.rem(x + k, NX)
        return xx, at(xx, z, core, grp)

    def z_peer(k):
        zz = lax.rem(z + k, NZ)
        return zz, at(x, zz, core, grp)

    def g_peer(k):
        gg = lax.rem(grp + k, G)
        return gg, at(x, z, core, gg)

    def copy(src, dst, s, r, dev):
        return pltpu.make_async_remote_copy(
            src_ref=src, dst_ref=dst, send_sem=s, recv_sem=r, device_id=dev, device_id_type=MESH
        )

    def rows(ref, start, count):
        return ref.at[pl.ds(pl.multiple_of(start, 16), count)]

    def iota(shape, axis):
        return lax.broadcasted_iota(jnp.int32, shape, axis)

    barrier = pltpu.get_barrier_semaphore()
    peers = [partner]
    peers += [x_peer(k)[1] for k in range(1, NX)]
    peers += [z_peer(k)[1] for k in range(1, NZ)]
    peers += [g_peer(k)[1] for k in range(1, G)]
    for dev in peers:
        pl.semaphore_signal(barrier, inc=1, device_id=dev, device_id_type=MESH)
    load_c = pltpu.make_async_copy(cache_ref, cvm, l_s.at[0])
    load_n = pltpu.make_async_copy(newl_ref, nvm, l_s.at[1])
    load_o = pltpu.make_async_copy(wo_ref, wov, l_s.at[2])
    load_c.start()

    to_row = dest_ref[0:1, :]
    spot_row = dest_ref[1:2, :]
    same = iota((NEW, NEW), 0) == iota((NEW, NEW), 1)
    to_col = jnp.sum(jnp.where(same, to_row, 0), axis=1, keepdims=True)
    spot_col = jnp.sum(jnp.where(same, spot_row, 0), axis=1, keepdims=True)
    here_row = to_row == grp
    hit = jnp.where((spot_row == iota((SLOTS, NEW), 0)) & here_row, 1, 0)
    left_col = 1 - jnp.sum(hit, axis=1, keepdims=True)

    def before(shape):
        slot = lax.rem(iota(shape, 1), SLOTS)
        return jnp.sum(jnp.where(iota(shape, 0) < slot, left_col, 0), axis=0, keepdims=True)

    def left(shape):
        slot = lax.rem(iota(shape, 1), SLOTS)
        return jnp.sum(jnp.where(iota(shape, 0) == slot, left_col, 0), axis=0, keepdims=True)

    before_t, left_t = before((SLOTS, TS)), left((SLOTS, TS))
    before_s, left_s = before((SLOTS, SLOTS)), left((SLOTS, SLOTS))
    is_surv = (before_s == iota((2 * R, SLOTS), 0)) & (left_s > 0) & (iota((2 * R, SLOTS), 0) < R)
    surv_col = jnp.sum(jnp.where(is_surv, iota((2 * R, SLOTS), 1), 0), axis=1, keepdims=True)
    idx_v[...] = jnp.broadcast_to(surv_col, idx_v.shape)
    fetch = pltpu.make_async_copy(idx_v, idx, l_s.at[3])
    fetch.start()
    row_of = iota((2 * R, NEW), 0) - R + grp * R
    is_mine = (iota((2 * R, NEW), 1) == row_of) & (iota((2 * R, NEW), 0) >= R)
    lens_col = jnp.sum(jnp.where(is_surv, clen_ref[...], 0), axis=1, keepdims=True) + jnp.sum(
        jnp.where(is_mine, plen_ref[...], 0), axis=1, keepdims=True
    )
    lens_v[...] = jnp.broadcast_to(lens_col, lens_v.shape)
    k_row, k_col = iota((NEW, NEW), 1), iota((NEW, NEW), 0)
    rank_row = jnp.sum(
        jnp.where((to_col == to_row) & (k_col // R == k_row // R) & (k_col < k_row), 1, 0),
        axis=0,
        keepdims=True,
    )
    i, j = iota((M, TS), 0), iota((M, TS), 1)
    sels[...] = jnp.where(
        (before_t == i // T) & (left_t > 0) & (j // SLOTS == i % T) & (i < RT), 1.0, 0.0
    ).astype(BF)
    i, j = iota((G * YP, NEW), 0), iota((G * YP, NEW), 1)
    u = i % YP
    from_k = jnp.where((j // R == i // YP) & here_row & (rank_row == u % PT // T), 1.0, 0.0)
    to_slot = jnp.where(spot_col == iota((NEW, TS), 1) % SLOTS, 1.0, 0.0)
    i, j = iota((G * YP, TS), 0), iota((G * YP, TS), 1)
    u = i % YP
    chosen = dot(from_k.astype(BF), to_slot.astype(BF))
    chosen = jnp.where(j // SLOTS == u % PT % T, chosen, 0.0)
    sely[...] = jnp.where(u < PT, chosen, 0.0).astype(BF)
    selh[...] = jnp.where((u >= PT) & (u < 2 * PT), chosen, 0.0).astype(BF)
    i, j = iota((M, NEW), 0), iota((M, NEW), 1)
    own_k = (j == (i - RT) // T + grp * R) & (i >= RT)
    key_col = jnp.sum(jnp.where(own_k, to_row * YP + rank_row * T, 0), axis=1, keepdims=True)
    i, j = iota((M, G * YP), 0), iota((M, G * YP), 1)
    pick[...] = jnp.where((key_col + i % T == j) & (i >= RT), 1.0, 0.0).astype(BF)
    xlo[...] = jnp.zeros(xlo.shape, BF)
    xhi[...] = jnp.zeros(xhi.shape, BF)
    xlo[:, :QA] = ql_ref[:, :QA]
    if QB:
        xhi[:, :QB] = ql_ref[:, QA:]
    xhi[:, QB : QB + KD] = nkv_ref[...]
    ysend[...] = (dot(sely[...], xlo[...]) + dot(selh[...], xhi[...])).astype(BF)
    half_dr = DR // 2
    lens_row = jnp.sum(
        jnp.where(iota((2 * R, 2 * R), 0) == iota((2 * R, 2 * R), 1), lens_col, 0),
        axis=0,
        keepdims=True,
    )

    def fresh_rows(count):
        i, j = iota((count, M), 0), iota((count, M), 1)
        low = jnp.where((j == i + RT) & (i < RT), 1.0, 0.0).astype(BF)
        low = dot(low, pick[...]).astype(BF)
        size = G * YP
        i, j = iota((size, size), 0), iota((size, size), 1)
        down = jnp.where(j == i + PT, 1.0, 0.0).astype(BF)
        return low, dot(low, down).astype(BF)

    def produce(half):
        i = iota((HM, 2 * R), 0)
        found = jnp.where((iota((HM, 2 * R), 1) == half * R + i // T) & (i < RT), lens_row, 0)
        pos = jnp.sum(found, axis=1, keepdims=True) + iota((HM, 1), 0) % T
        angle = pos.astype(F32) * freq_ref[...]
        cos, sin = jnp.cos(angle), jnp.sin(angle)
        sin = jnp.where(iota((HM, DR), 1) < half_dr, -sin, sin)
        if half == 0:
            xin = dot(sels[:HM, :], ql_ref[...]).astype(BF)
            qf = dot(xin, wuq_ref[...])
        else:
            low, high = fresh_rows(HM)
            qf = dot(dot(low, yrecv[:, :QA]).astype(BF), wuq_ref[:QA, :])
            if QB:
                qf = qf + dot(dot(high, yrecv[:, :QB]).astype(BF), wuq_ref[QA:, :])
        qf = qf.astype(BF)
        HD = DN + DR
        for h in range(HL):
            nope = dot(qf, onehot(HL * HD, DN, lambda i: i - h * HD).astype(BF)).astype(BF)
            qh[h, :, :DL] = dot(nope, wuk_ref[h]).astype(BF)
            turned = lambda i: jnp.where(
                (i >= h * HD + DN) & (i < (h + 1) * HD), (i - h * HD - DN + half_dr) % DR, -1
            )
            rot = dot(qf, onehot(HL * HD, DR, lambda i: i - h * HD - DN).astype(BF))
            swp = dot(qf, onehot(HL * HD, DR, turned).astype(BF))
            qh[h, :, DL:] = (rot * cos + swp * sin).astype(BF)
        total = None
        for h in range(HL):
            sel = onehot(
                HL * RT,
                HM,
                lambda i: jnp.where((i >= h * RT) & (i < (h + 1) * RT), i - h * RT, -1),
            ).astype(BF)
            term = dot(sel, qh[h])
            total = term if total is None else total + term
        return total.astype(BF)

    pl.semaphore_wait(barrier, len(peers))
    done = []
    for k in range(1, G):
        gg, dev = g_peer(k)
        c = copy(rows(ysend, gg * YP, YP), rows(yrecv, grp * YP, YP), y_s.at[k], y_r.at[grp], dev)
        c.start()
        done.append(c)
    own = pl.ds(pl.multiple_of(grp * YP, 16), YP)
    yrecv[own, :] = ysend[own, :]

    keys = copy(kx, ko, p_s.at[0], p_r.at[0], partner)
    done.append(keys)

    @pl.when(core == 0)
    def _():
        copy(newl_ref, ko, p_s.at[0], p_r.at[0], partner).start()

    fetch.wait()
    load_c.wait()

    @pl.when(core == 1)
    def _():
        for j in range(R):
            kx[j] = cvm[idx[j, 0]]
        keys.start()
        load_n.start()

    load_o.start()

    def incoming():
        for k in range(1, G):
            gg, dev = g_peer(k)
            copy(
                rows(ysend, gg * YP, YP), rows(yrecv, gg * YP, YP), y_s.at[k], y_r.at[gg], dev
            ).wait_recv()

    def to_partner(block):
        qsend[...] = block
        c = copy(qsend, pq.at[core], p_s.at[1], p_r.at[1], partner)
        c.start()

    def gather_chunk():
        copy(qsend, pq.at[1 - core], p_s.at[1], p_r.at[1], partner).wait_recv()
        regroup = onehot(
            CH, CH, lambda i: i % (2 * HL) * RT + i // QC * T + i % QC // (2 * HL)
        ).astype(BF)
        ck[...] = (dot(regroup, pq[...].reshape(CH, KD))).astype(BF)

    done.append(copy(qsend, pq.at[core], p_s.at[1], p_r.at[1], partner))

    def spread(cc, n1, i1, peer1, n2, i2, peer2):
        w = n1 * QC
        blk = R * w
        sub = RQ * w
        sends = []

        def hops(n, b, d):
            return n // 2 if (b == 0) == (d == 0) else n - 1 - n // 2

        def ring(n, i, d, k):
            return lax.rem(i + (k if d == 0 else n - k), n)

        part_rows = CH // 2

        def cell(o2, o1, b):
            return rows(qall, (o2 * n1 + o1) * CH + b * part_rows, part_rows)

        def new_at(s):
            if s == 0:
                return [(b, i1, None) for b in range(2)]
            return [
                (b, ring(n1, i1, 1 - d, s), d)
                for b in range(2)
                for d in range(2)
                if s <= hops(n1, b, d)
            ]

        def first_copy(b, o1, d, h):
            _, dev = peer1(1 if d == 0 else n1 - 1)
            here = cell(i2, o1, b)
            return copy(here, here, a1_s.at[b, d, h], a1_r.at[b, o1], dev)

        def second_copy(b, o1, o2, d, h):
            _, dev = peer2(1 if d == 0 else n2 - 1)
            here = cell(o2, o1, b)
            return copy(here, here, a2_s.at[b, o1, d, h], a2_r.at[b, o1, o2], dev)

        def launch(c):
            c.start()
            sends.append(c)

        def gather_step(s):
            if s <= n1 // 2:
                for b, o1, d in new_at(s):
                    if s:
                        first_copy(b, o1, d, s).wait_recv()
                    for way in (0, 1) if d is None else (d,):
                        if s + 1 <= hops(n1, b, way):
                            launch(first_copy(b, o1, way, s + 1))
                    for way in range(2):
                        if hops(n2, b, way):
                            launch(second_copy(b, o1, i2, way, 1))
            for h in range(2, n2 // 2 + 1):
                if not 0 <= s - h + 1 <= n1 // 2:
                    continue
                for b, o1, _ in new_at(s - h + 1):
                    for way in range(2):
                        if h <= hops(n2, b, way):
                            o2 = ring(n2, i2, 1 - way, h - 1)
                            c = second_copy(b, o1, o2, way, h)
                            c.wait_recv()
                            launch(c)

        def settle(b):
            for k1 in range(n1):
                o1 = lax.rem(i1 + k1, n1)
                for k2 in range(1, n2):
                    o2 = lax.rem(i2 + k2, n2)
                    way = 1 if k2 <= hops(n2, b, 1) else 0
                    dist = k2 if way == 1 else n2 - k2
                    if dist == hops(n2, b, way):
                        second_copy(b, o1, o2, way, dist).wait_recv()

        if cc == 0:
            pq[0] = produce(0)
        else:
            to_partner(produce(0))
            incoming()
            pq[1] = produce(1)
        gather_chunk()
        qall[pl.ds(pl.multiple_of((i2 * n1 + i1) * CH, 16), CH), :] = ck[...]
        gather_step(0)
        if cc == 0:
            incoming()
            to_partner(produce(1))
        for s in range(1, n1 // 2 + max(1, n2 // 2)):
            gather_step(s)

        many = min(4, n1)
        span = many * QC
        mix = onehot(
            RB * span,
            RB * span,
            lambda i: i % span // QC * part_rows + i // span * QC + i % QC,
        ).astype(BF)

        def pack(b):
            def one(g, _):
                source = jnp.concatenate(
                    [
                        qall[
                            pl.ds(
                                pl.multiple_of((g * many + o) * CH + b * part_rows, 16), part_rows
                            ),
                            :,
                        ]
                        for o in range(many)
                    ],
                    0,
                )
                mixed = dot(mix, source).astype(BF)
                for r in range(RB):
                    here = pl.ds(pl.multiple_of(r * nq + g * span, 8), span)
                    qp[here, :] = mixed[r * span : (r + 1) * span]
                return 0

            lax.fori_loop(0, n1 * n2 // many, one, 0)

        nq = n2 * w
        big = n2 // 2
        copy(kx, ko, p_s.at[0], p_r.at[0], partner).wait_recv()
        if cc == 1:
            load_n.wait()

        st[...] = jnp.full(st.shape, NEG, F32)
        def attend(r, _):
            q = qp[pl.ds(pl.multiple_of(lax.rem(r, RB) * nq, 16), nq), :]
            if cc == 0:
                k_a, k_b = cvm[idx[r, 0]], ko[r]
            else:
                k_a, k_b = ko[r], nvm[r]
            mine = jnp.where(iota(lens_v.shape, 0) == r + cc * R, lens_v[...], 0)
            length = jnp.sum(mine, axis=0, keepdims=True)[:, :1]
            base = (shard - core) * seq
            place = base + lax.broadcasted_iota(jnp.int32, (nq, seq), 1)
            ok_a, ok_b = place < length, place + seq < length
            s_a = jnp.where(ok_a, dot(q, k_a) * scale, NEG)
            s_b = jnp.where(ok_b, dot(q, k_b) * scale, NEG)
            top = jnp.maximum(
                jnp.max(s_a, axis=1, keepdims=True), jnp.max(s_b, axis=1, keepdims=True)
            )
            p_a = jnp.where(ok_a, jnp.exp(s_a - top), 0.0)
            p_b = jnp.where(ok_b, jnp.exp(s_b - top), 0.0)
            total = jnp.sum(p_a, axis=1, keepdims=True) + jnp.sum(p_b, axis=1, keepdims=True)
            summed = dot_t(p_a.astype(BF), k_a[:DL, :]) + dot_t(p_b.astype(BF), k_b[:DL, :])
            some = total > 0.0
            safe = jnp.where(some, total, 1.0)
            value = (summed * (1.0 / safe)).astype(BF)
            lse = jnp.where(some, top + jnp.log(safe), NEG)
            for o in range(n2):
                acc[pl.ds(pl.multiple_of(o * blk + r * w, 16), w), :] = value[o * w : (o + 1) * w]
                column = jnp.where(iota((w, 128), 0) == iota((w, 128), 1), lse[o * w : (o + 1) * w], 0.0)
                line = jnp.sum(column, axis=0, keepdims=True)
                st[r // RQ, o] = jnp.where(iota((R, 128), 0) == r, line, st[r // RQ, o])
            return 0

        def slot(q, d, h):
            return q * (n2 - 1) + (0 if d == 0 else hops(n2, q % 2, 0)) + h - 1

        def merge(q, target, slots):
            parts = [st[q, target]] + [rss[s] for s in slots]
            top = functools.reduce(jnp.maximum, parts)
            weights = [jnp.exp(p - top) for p in parts]
            total = functools.reduce(jnp.add, weights)
            weights = [v / total for v in weights]
            st[q, target] = top + jnp.log(total)
            same = iota((w, 128), 0) == iota((w, 128), 1)
            for r in range(RQ):
                mine = pl.ds(pl.multiple_of(target * blk + q * sub + r * w, 16), w)
                values = [acc[mine, :]]
                for s in slots:
                    values.append(rsr[pl.ds(s * sub + r * w, w), :])
                out = None
                row = q * RQ + r
                for v, g in zip(values, weights):
                    col = jnp.sum(jnp.where(same, g[row : row + 1, :], 0.0), axis=1, keepdims=True)
                    term = v.astype(F32) * col
                    out = term if out is None else out + term
                acc[mine, :] = out.astype(BF)

        def reduce_copies(q, d, h, target, dev):
            s = slot(q, d, h)
            big_copy = copy(
                rows(acc, target * blk + q * sub, sub),
                rsr.at[pl.ds(s * sub, sub)],
                c_s.at[q, d, h],
                c_r.at[q, d, h],
                dev,
            )
            small_copy = copy(
                st.at[q, target], rss.at[s], d_s.at[q, d, h], d_r.at[q, d, h], dev
            )
            return big_copy, small_copy

        def step(q, d, h):
            if h > hops(n2, q % 2, d):
                return
            _, dev = peer2(1 if d == 0 else n2 - 1)
            target = ring(n2, i2, d, hops(n2, q % 2, d) - h + 1)
            if h > 1:
                for c in reduce_copies(q, d, h - 1, target, dev):
                    c.wait_recv()
                merge(q, target, [slot(q, d, h - 1)])
            for c in reduce_copies(q, d, h, target, dev):
                launch(c)

        for b in range(2):
            settle(b)
            pack(b)
            for q in (2 * b, 2 * b + 1):
                lax.fori_loop(q * RQ, (q + 1) * RQ, attend, 0)
                for d in range(2):
                    step(q, d, 1)
        for h in range(2, big + 1):
            for q in range(4):
                for d in range(2):
                    step(q, d, h)

        for b in range(2):
            for q in (2 * b, 2 * b + 1):
                slots = []
                for d in range(2):
                    last = hops(n2, q % 2, d)
                    if last:
                        _, dev = peer2(1 if d == 0 else n2 - 1)
                        for c in reduce_copies(q, d, last, i2, dev):
                            c.wait_recv()
                        slots.append(slot(q, d, last))
                if slots:
                    merge(q, i2, slots)
            block = pl.ds(pl.multiple_of(i2 * blk + 2 * b * sub, 16), 2 * sub)
            for k in range(1, n1 + 1):
                j, dev = peer1(k)
                sel = onehot(part_rows, 2 * sub, lambda i: i // QC * w + j * QC + i % QC)
                value = dot(sel.astype(BF), acc[block, :]).astype(BF)
                if k == n1:
                    rb[pl.ds(pl.multiple_of(i1 * CH + b * part_rows, 16), part_rows), :] = value
                    continue
                sb[k, b * part_rows : (b + 1) * part_rows] = value
                launch(
                    copy(
                        sb.at[k, pl.ds(b * part_rows, part_rows)],
                        rows(rb, i1 * CH + b * part_rows, part_rows),
                        e_s.at[k, b],
                        e_r.at[i1, b],
                        dev,
                    )
                )
        stats = st[0, i2]
        for q in range(1, 4):
            stats = jnp.where(iota((R, 128), 0) // RQ == q, st[q, i2], stats)
        for k in range(1, n1 + 1):
            j, dev = peer1(k)
            sel = onehot(128, 128, lambda i: jnp.where(i // QC == j, i % QC, -1))
            stat = dot(stats, sel, precision=lax.Precision.HIGHEST)
            if k == n1:
                rst[i1] = stat
                continue
            sst[k] = stat
            launch(copy(sst.at[k], rst.at[i1], f_s.at[k], f_r.at[i1], dev))
        for k in range(1, n1):
            j, dev = peer1(k)
            for b in range(2):
                copy(
                    sb.at[k, pl.ds(b * part_rows, part_rows)],
                    rows(rb, j * CH + b * part_rows, part_rows),
                    e_s.at[k, b],
                    e_r.at[j, b],
                    dev,
                ).wait_recv()
            copy(sst.at[k], rst.at[j], f_s.at[k], f_r.at[j], dev).wait_recv()

        if cc == 0:
            nkv = dot(sels[...], nkv_ref[...]).astype(BF)
        else:
            nkv = dot(fresh_rows(M)[1], yrecv[:, QB : QB + KD]).astype(BF)
        fresh = dot_t(ck[...], nkv) * scale
        i = lax.broadcasted_iota(jnp.int32, (CH, M), 0)
        j = lax.broadcasted_iota(jnp.int32, (CH, M), 1)
        seen = (i // QC == j // T) & (j % T <= i % QC // (2 * HL)) & (j < RT)
        fresh = jnp.where(seen, fresh, NEG)
        fill = onehot(CH, R, lambda i: i // QC)
        own_head = lax.broadcasted_iota(jnp.int32, (CH, 128), 0) % QC
        lane = lax.broadcasted_iota(jnp.int32, (CH, 128), 1)
        lses = []
        for s in range(n1):
            spread_out = dot(fill, rst[s], precision=lax.Precision.HIGHEST)
            lses.append(
                jnp.sum(jnp.where(lane == own_head, spread_out, 0.0), axis=1, keepdims=True)
            )
        top = functools.reduce(jnp.maximum, lses, jnp.max(fresh, axis=1, keepdims=True))
        probs = jnp.where(seen, jnp.exp(fresh - top), 0.0)
        total = jnp.sum(probs, axis=1, keepdims=True)
        summed = dot(probs.astype(BF), nkv[:, :DL])
        for s in range(n1):
            g = jnp.exp(lses[s] - top)
            total = total + g
            summed = summed + rb[s * CH : (s + 1) * CH, :].astype(F32) * g
        lat[...] = (summed / total).astype(BF)
        for c in sends:
            c.wait_send()

    @pl.when(core == 0)
    def _():
        spread(0, NX, x, x_peer, NZ, z, z_peer)

    @pl.when(core == 1)
    def _():
        spread(1, NZ, z, z_peer, NX, x, x_peer)

    def heads_of(cc):
        sel = onehot(
            HL * RT,
            CH,
            lambda i: i % RT // T * QC + i % T * (2 * HL) + cc * HL + i // RT,
        ).astype(BF)
        return dot(sel, lat[...]).astype(BF)

    fl[...] = heads_of(1 - core)
    swap = copy(fl, lo.at[core], p_s.at[2], p_r.at[2], partner)
    swap.start()
    done.append(swap)
    lo[core] = heads_of(core)
    copy(fl, lo.at[1 - core], p_s.at[2], p_r.at[2], partner).wait_recv()
    every = lo[...].reshape(2 * HL * RT, DL)
    flat = []
    for h in range(HL):
        value = dot(every, wuv_ref[h]).astype(BF)
        sel = onehot(M, 2 * HL * RT, lambda i: i // RT * (HL * RT) + h * RT + i % RT).astype(BF)
        flat.append(dot(sel, value).astype(BF))
    flat = jnp.concatenate(flat, 1)
    load_o.wait()
    part[...] = dot(flat, wov[...])
    shards = 2 * NX * NZ
    for s in range(shards):
        s_pre, rest = divmod(s, 2 * NZL * NX)
        s_x, rest = divmod(rest, 2 * NZL)
        s_zl, s_core = divmod(rest, 2)
        first = s * W // 128
        off = s * W - first * 128
        if off + W <= 128:
            piece = part[:, first * 128 : (first + 1) * 128]
            if off:
                piece = pltpu.roll(piece, 128 - off, 1)
        else:
            piece = pltpu.roll(part[:, first * 128 : (first + 2) * 128], 256 - off, 1)[:, :128]
        po[s_core, s_x, s_pre * NZL + s_zl] = piece
    swap = copy(po.at[1 - core], pr, p_s.at[3], p_r.at[3], partner)
    swap.start()
    done.append(swap)
    swap.wait_recv()
    po[core] = po[core] + pr[...]
    for k in range(1, NX):
        j, dev = x_peer(k)
        xs[k] = po[core, j].astype(BF)
        c = copy(xs.at[k], xr.at[x], x_s.at[k], x_r.at[x], dev)
        c.start()
        done.append(c)
    total = po[core, x]
    for k in range(1, NX):
        j, dev = x_peer(k)
        copy(xs.at[k], xr.at[j], x_s.at[k], x_r.at[j], dev).wait_recv()
        total = total + xr[j].astype(F32)
    zs[...] = total
    for k in range(1, NZ):
        j, dev = z_peer(k)
        c = copy(zs.at[j], zr.at[z], z_s.at[k], z_r.at[z], dev)
        c.start()
        done.append(c)
    total = zs[z]
    for k in range(1, NZ):
        j, dev = z_peer(k)
        copy(zs.at[j], zr.at[j], z_s.at[k], z_r.at[j], dev).wait_recv()
        total = total + zr[j]
    final = total.astype(BF)
    yos[...] = dot_c(pick[...], final).astype(BF)
    for k in range(1, G):
        gg, dev = g_peer(k)
        c = copy(rows(yos, gg * YP, YP), rows(yor, grp * YP, YP), o_s.at[k], o_r.at[grp], dev)
        c.start()
        done.append(c)
    yor[own, :] = yos[own, :]
    for k in range(1, G):
        gg, dev = g_peer(k)
        copy(
            rows(yos, gg * YP, YP), rows(yor, gg * YP, YP), o_s.at[k], o_r.at[gg], dev
        ).wait_recv()
    placed = dot_c(sels[...], final) + dot_c(sely[...], yor[...])
    out_ref[...] = placed[:, :W].astype(BF)
    for c in done:
        c.wait_send()


def local(sizes, cache, cache_len, new_latent, prompt_len, dest, q_latent, new_kv, w_uq, w_uk, w_uv, w_o):
    G, NX, NZ, NZL = sizes
    rows_n, seq, KD = cache.shape
    T, _, QL = q_latent.shape
    HL, DN, DL = w_uk.shape
    DR = KD - DL
    R = new_latent.shape[0]
    PERG = R // G
    YP = up(2 * PERG * T, 16)
    shards = 2 * NX * NZ
    W = w_o.shape[1] // shards
    M = 2 * R * T
    HM = up(R * T, 16)
    QC = T * 2 * HL
    CH = R * QC
    nq = NX * NZ * QC
    KP = up(KD, 128)
    QA = min(QL, up((QL + KP) // 2, 128))
    YW = max(QA, QL - QA + KP)
    half = DR // 2
    freq = ROPE_BASE ** (-jnp.arange(half, dtype=F32) / half)
    freq = jnp.concatenate([freq, freq])[None, :]
    dims = (G, NX, NZ, NZL, T, R, HL, PERG, YP, KD, DL, DN, DR, QL, W, rows_n, QA)
    tall = max(NX, NZ)

    def slots_rows(n1, n2, per):
        return 2 * (n2 - 1) * n1 * QC * per

    rsr_rows = max(slots_rows(NX, NZ, R // 2), slots_rows(NZ, NX, R // 2), 16)
    hop = tall // 2 + 1
    vmem = pl.BlockSpec(memory_space=pltpu.VMEM)
    anywhere = pl.BlockSpec(memory_space=pl.ANY)
    dma = pltpu.SemaphoreType.DMA
    V = pltpu.VMEM
    out = pl.pallas_call(
        functools.partial(kernel, dims),
        out_shape=jax.ShapeDtypeStruct((T * rows_n, W), BF),
        in_specs=[vmem] * 9 + [anywhere] * 3,
        out_specs=vmem,
        scratch_shapes=[
            V((rows_n, KD, seq), BF),
            V((R, KD, seq), BF),
            V(w_o.shape, BF),
            V((2 * R, 128), jnp.int32),
            pltpu.SMEM((2 * R, 128), jnp.int32),
            V((2 * R, 128), jnp.int32),
            V((M, T * rows_n), BF),
            V((G * YP, T * rows_n), BF),
            V((G * YP, T * rows_n), BF),
            V((M, G * YP), BF),
            V((T * rows_n, YW), BF),
            V((T * rows_n, YW), BF),
            V((G * YP, YW), BF),
            V((G * YP, YW), BF),
            V((R, KD, seq), BF),
            V((R, KD, seq), BF),
            V((HL, HM, KD), BF),
            V((HL * R * T, KD), BF),
            V((2, HL * R * T, KD), BF),
            V((CH, KD), BF),
            V((NX * NZ * CH, KD), BF),
            V((R // 2 * nq, KD), BF),
            V((R * nq, DL), BF),
            V((rsr_rows, DL), BF),
            V((4, tall, R, 128), F32),
            V((4 * (tall - 1), R, 128), F32),
            V((tall, CH, DL), BF),
            V((tall, R, 128), F32),
            V((tall * CH, DL), BF),
            V((tall, R, 128), F32),
            V((CH, DL), BF),
            V((2, HL * R * T, DL), BF),
            V((HL * R * T, DL), BF),
            V((M, shards * W), F32),
            V((2, NX, NZ, M, 128), F32),
            V((NX, NZ, M, 128), F32),
            V((NX, NZ, M, 128), BF),
            V((NX, NZ, M, 128), BF),
            V((NZ, M, 128), F32),
            V((NZ, M, 128), F32),
            V((G * YP, 128), BF),
            V((G * YP, 128), BF),
            dma((4,)), dma((G,)), dma((G,)), dma((4,)), dma((4,)),
            dma((2, 2, hop)), dma((2, tall)), dma((2, tall, 2, hop)), dma((2, tall, tall)),
            dma((4, 2, hop)), dma((4, 2, hop)), dma((4, 2, hop)), dma((4, 2, hop)),
            dma((tall, 2)), dma((tall, 2)), dma((tall,)), dma((tall,)),
            dma((NX,)), dma((NX,)), dma((NZ,)), dma((NZ,)), dma((G,)), dma((G,)),
        ],
        compiler_params=pltpu.CompilerParams(
            collective_id=0, has_side_effects=True, vmem_limit_bytes=60 * 2**20
        ),
    )(
        dest.T,
        cache_len[None, :],
        prompt_len[None, :],
        freq,
        q_latent.reshape(T * rows_n, QL),
        new_kv.reshape(T * rows_n, KD),
        w_uq,
        w_uk,
        w_uv,
        cache.transpose(0, 2, 1),
        new_latent.transpose(0, 2, 1),
        w_o,
    )
    return out.reshape(T, rows_n, W)


def solution(mesh):
    placed = (
        P("grp", ("pre", "dec"), None),
        P("grp"),
        P("grp", ("pre", "dec"), None),
        P(),
        P(),
        P(None, "grp", None),
        P(None, "grp", None),
        P(None, ("pre", "dec")),
        P(("pre", "dec"), None, None),
        P(("pre", "dec"), None, None),
        P(("pre", "dec"), None),
    )
    zl = 2
    sizes = (
        mesh.shape["grp"],
        mesh.shape["dec"] // (2 * zl),
        mesh.shape["pre"] * zl,
        zl,
    )
    return jax.shard_map(
        functools.partial(local, sizes),
        mesh=mesh,
        in_specs=placed,
        out_specs=P(None, "grp", ("pre", "dec")),
        check_vma=False,
    )
```

```python
import functools
import math

import jax
import jax.numpy as jnp
from jax import lax
from jax.experimental import pallas as pl
from jax.experimental.pallas import tpu as pltpu
from jax.sharding import PartitionSpec as P

ROPE_BASE = 10000.0
MESH = pl.DeviceIdType.MESH
NEG = -1e30
BF = jnp.bfloat16
F32 = jnp.float32


def up(value, unit):
    return -(-value // unit) * unit


def dot(a, b, **kw):
    return jnp.dot(a, b, preferred_element_type=F32, **kw)


def dot_t(a, b):
    return lax.dot_general(a, b, (((1,), (1,)), ((), ())), preferred_element_type=F32)


def dot_c(a, b):
    return lax.dot_general(a, b, (((0,), (0,)), ((), ())), preferred_element_type=F32)


def onehot(rows, cols, source):
    i = lax.broadcasted_iota(jnp.int32, (rows, cols), 0)
    j = lax.broadcasted_iota(jnp.int32, (rows, cols), 1)
    return jnp.where(source(i) == j, 1.0, 0.0)


def kernel(
    dims,
    dest_ref, clen_ref, plen_ref, freq_ref, ql_ref, nkv_ref, wuq_ref, wuk_ref, wuv_ref,
    cache_ref, newl_ref, wo_ref,
    out_ref,
    cvm, nvm, wov, idx_v, idx, lens_v, sels, sely, selh, pick, xlo, xhi,
    ysend, yrecv, kx, ko, qh, qsend, pq, ck, qall, qp, acc, rsr, st, rss,
    sb, sst, rb, rst, lat, lo, fl, part, po, pr, xs, xr, zs, zr, yos, yor,
    l_s, y_s, y_r, p_s, p_r, a1_s, a1_r, a2_s, a2_r, c_s, c_r, d_s, d_r,
    e_s, e_r, f_s, f_r, x_s, x_r, z_s, z_r, o_s, o_r, w_s, w_r,
):
    G, NX, NZ, NZL, T, R, HL, PERG, YP, KD, DL, DN, DR, QL, W, SLOTS, QA = dims
    QC = T * 2 * HL
    CH = R * QC
    RT = R * T
    M = 2 * RT
    HM = up(RT, 16)
    RB = R // 2
    RQ = R // 4
    QB = QL - QA
    NEW = G * R
    TS = T * SLOTS
    PT = PERG * T
    scale = 1.0 / math.sqrt(DN + DR)
    seq = cache_ref.shape[2]
    pre, grp, dec = lax.axis_index("pre"), lax.axis_index("grp"), lax.axis_index("dec")
    core = lax.rem(dec, 2)
    z = pre * NZL + lax.rem(dec // 2, NZL)
    x = dec // (2 * NZL)
    shard = pre * (2 * NZL * NX) + dec

    def at(xx, zz, cc, gg):
        return (zz // NZL, gg, xx * (2 * NZL) + lax.rem(zz, NZL) * 2 + cc)

    partner = at(x, z, 1 - core, grp)

    def x_peer(k):
        xx = lax.rem(x + k, NX)
        return xx, at(xx, z, core, grp)

    def z_peer(k):
        zz = lax.rem(z + k, NZ)
        return zz, at(x, zz, core, grp)

    def g_peer(k):
        gg = lax.rem(grp + k, G)
        return gg, at(x, z, core, gg)

    def copy(src, dst, s, r, dev):
        return pltpu.make_async_remote_copy(
            src_ref=src, dst_ref=dst, send_sem=s, recv_sem=r, device_id=dev, device_id_type=MESH
        )

    def rows(ref, start, count):
        return ref.at[pl.ds(pl.multiple_of(start, 16), count)]

    def iota(shape, axis):
        return lax.broadcasted_iota(jnp.int32, shape, axis)

    barrier = pltpu.get_barrier_semaphore()
    peers = [partner]
    peers += [x_peer(k)[1] for k in range(1, NX)]
    peers += [z_peer(k)[1] for k in range(1, NZ)]
    peers += [g_peer(k)[1] for k in range(1, G)]
    for dev in peers:
        pl.semaphore_signal(barrier, inc=1, device_id=dev, device_id_type=MESH)
    load_c = pltpu.make_async_copy(cache_ref, cvm, l_s.at[0])
    load_n = pltpu.make_async_copy(newl_ref, nvm, l_s.at[1])
    load_o = pltpu.make_async_copy(wo_ref, wov, l_s.at[2])
    load_c.start()

    to_row = dest_ref[0:1, :]
    spot_row = dest_ref[1:2, :]
    same = iota((NEW, NEW), 0) == iota((NEW, NEW), 1)
    to_col = jnp.sum(jnp.where(same, to_row, 0), axis=1, keepdims=True)
    spot_col = jnp.sum(jnp.where(same, spot_row, 0), axis=1, keepdims=True)
    here_row = to_row == grp
    hit = jnp.where((spot_row == iota((SLOTS, NEW), 0)) & here_row, 1, 0)
    left_col = 1 - jnp.sum(hit, axis=1, keepdims=True)

    def before(shape):
        slot = lax.rem(iota(shape, 1), SLOTS)
        return jnp.sum(jnp.where(iota(shape, 0) < slot, left_col, 0), axis=0, keepdims=True)

    def left(shape):
        slot = lax.rem(iota(shape, 1), SLOTS)
        return jnp.sum(jnp.where(iota(shape, 0) == slot, left_col, 0), axis=0, keepdims=True)

    before_t, left_t = before((SLOTS, TS)), left((SLOTS, TS))
    before_s, left_s = before((SLOTS, SLOTS)), left((SLOTS, SLOTS))
    is_surv = (before_s == iota((2 * R, SLOTS), 0)) & (left_s > 0) & (iota((2 * R, SLOTS), 0) < R)
    surv_col = jnp.sum(jnp.where(is_surv, iota((2 * R, SLOTS), 1), 0), axis=1, keepdims=True)
    idx_v[...] = jnp.broadcast_to(surv_col, idx_v.shape)
    fetch = pltpu.make_async_copy(idx_v, idx, l_s.at[3])
    fetch.start()
    row_of = iota((2 * R, NEW), 0) - R + grp * R
    is_mine = (iota((2 * R, NEW), 1) == row_of) & (iota((2 * R, NEW), 0) >= R)
    lens_col = jnp.sum(jnp.where(is_surv, clen_ref[...], 0), axis=1, keepdims=True) + jnp.sum(
        jnp.where(is_mine, plen_ref[...], 0), axis=1, keepdims=True
    )
    lens_v[...] = jnp.broadcast_to(lens_col, lens_v.shape)
    k_row, k_col = iota((NEW, NEW), 1), iota((NEW, NEW), 0)
    rank_row = jnp.sum(
        jnp.where((to_col == to_row) & (k_col // R == k_row // R) & (k_col < k_row), 1, 0),
        axis=0,
        keepdims=True,
    )
    i, j = iota((M, TS), 0), iota((M, TS), 1)
    sels[...] = jnp.where(
        (before_t == i // T) & (left_t > 0) & (j // SLOTS == i % T) & (i < RT), 1.0, 0.0
    ).astype(BF)
    i, j = iota((G * YP, NEW), 0), iota((G * YP, NEW), 1)
    u = i % YP
    from_k = jnp.where((j // R == i // YP) & here_row & (rank_row == u % PT // T), 1.0, 0.0)
    to_slot = jnp.where(spot_col == iota((NEW, TS), 1) % SLOTS, 1.0, 0.0)
    i, j = iota((G * YP, TS), 0), iota((G * YP, TS), 1)
    u = i % YP
    chosen = dot(from_k.astype(BF), to_slot.astype(BF))
    chosen = jnp.where(j // SLOTS == u % PT % T, chosen, 0.0)
    sely[...] = jnp.where(u < PT, chosen, 0.0).astype(BF)
    selh[...] = jnp.where((u >= PT) & (u < 2 * PT), chosen, 0.0).astype(BF)
    i, j = iota((M, NEW), 0), iota((M, NEW), 1)
    own_k = (j == (i - RT) // T + grp * R) & (i >= RT)
    key_col = jnp.sum(jnp.where(own_k, to_row * YP + rank_row * T, 0), axis=1, keepdims=True)
    i, j = iota((M, G * YP), 0), iota((M, G * YP), 1)
    pick[...] = jnp.where((key_col + i % T == j) & (i >= RT), 1.0, 0.0).astype(BF)
    xlo[...] = jnp.zeros(xlo.shape, BF)
    xhi[...] = jnp.zeros(xhi.shape, BF)
    xlo[:, :QA] = ql_ref[:, :QA]
    if QB:
        xhi[:, :QB] = ql_ref[:, QA:]
    xhi[:, QB : QB + KD] = nkv_ref[...]
    ysend[...] = (dot(sely[...], xlo[...]) + dot(selh[...], xhi[...])).astype(BF)
    half_dr = DR // 2
    lens_row = jnp.sum(
        jnp.where(iota((2 * R, 2 * R), 0) == iota((2 * R, 2 * R), 1), lens_col, 0),
        axis=0,
        keepdims=True,
    )

    def fresh_rows(count):
        i, j = iota((count, M), 0), iota((count, M), 1)
        low = jnp.where((j == i + RT) & (i < RT), 1.0, 0.0).astype(BF)
        low = dot(low, pick[...]).astype(BF)
        size = G * YP
        i, j = iota((size, size), 0), iota((size, size), 1)
        down = jnp.where(j == i + PT, 1.0, 0.0).astype(BF)
        return low, dot(low, down).astype(BF)

    def produce(half):
        i = iota((HM, 2 * R), 0)
        found = jnp.where((iota((HM, 2 * R), 1) == half * R + i // T) & (i < RT), lens_row, 0)
        pos = jnp.sum(found, axis=1, keepdims=True) + iota((HM, 1), 0) % T
        angle = pos.astype(F32) * freq_ref[...]
        cos, sin = jnp.cos(angle), jnp.sin(angle)
        sin = jnp.where(iota((HM, DR), 1) < half_dr, -sin, sin)
        if half == 0:
            xin = dot(sels[:HM, :], ql_ref[...]).astype(BF)
            qf = dot(xin, wuq_ref[...])
        else:
            low, high = fresh_rows(HM)
            qf = dot(dot(low, yrecv[:, :QA]).astype(BF), wuq_ref[:QA, :])
            if QB:
                qf = qf + dot(dot(high, yrecv[:, :QB]).astype(BF), wuq_ref[QA:, :])
        qf = qf.astype(BF)
        HD = DN + DR
        for h in range(HL):
            nope = dot(qf, onehot(HL * HD, DN, lambda i: i - h * HD).astype(BF)).astype(BF)
            qh[h, :, :DL] = dot(nope, wuk_ref[h]).astype(BF)
            turned = lambda i: jnp.where(
                (i >= h * HD + DN) & (i < (h + 1) * HD), (i - h * HD - DN + half_dr) % DR, -1
            )
            rot = dot(qf, onehot(HL * HD, DR, lambda i: i - h * HD - DN).astype(BF))
            swp = dot(qf, onehot(HL * HD, DR, turned).astype(BF))
            qh[h, :, DL:] = (rot * cos + swp * sin).astype(BF)
        total = None
        for h in range(HL):
            sel = onehot(
                HL * RT,
                HM,
                lambda i: jnp.where((i >= h * RT) & (i < (h + 1) * RT), i - h * RT, -1),
            ).astype(BF)
            term = dot(sel, qh[h])
            total = term if total is None else total + term
        return total.astype(BF)

    pl.semaphore_wait(barrier, len(peers))
    done = []
    for k in range(1, G):
        gg, dev = g_peer(k)
        c = copy(rows(ysend, gg * YP, YP), rows(yrecv, grp * YP, YP), y_s.at[k], y_r.at[grp], dev)
        c.start()
        done.append(c)
    own = pl.ds(pl.multiple_of(grp * YP, 16), YP)
    yrecv[own, :] = ysend[own, :]

    keys = copy(kx, ko, p_s.at[0], p_r.at[0], partner)
    done.append(keys)

    @pl.when(core == 0)
    def _():
        copy(newl_ref, ko, p_s.at[0], p_r.at[0], partner).start()

    fetch.wait()
    load_c.wait()

    @pl.when(core == 1)
    def _():
        for j in range(R):
            kx[j] = cvm[idx[j, 0]]
        keys.start()
        load_n.start()

    load_o.start()

    def incoming():
        for k in range(1, G):
            gg, dev = g_peer(k)
            copy(
                rows(ysend, gg * YP, YP), rows(yrecv, gg * YP, YP), y_s.at[k], y_r.at[gg], dev
            ).wait_recv()

    def to_partner(block):
        qsend[...] = block
        c = copy(qsend, pq.at[core], p_s.at[1], p_r.at[1], partner)
        c.start()

    def gather_chunk():
        copy(qsend, pq.at[1 - core], p_s.at[1], p_r.at[1], partner).wait_recv()
        regroup = onehot(
            CH, CH, lambda i: i % (2 * HL) * RT + i // QC * T + i % QC // (2 * HL)
        ).astype(BF)
        ck[...] = (dot(regroup, pq[...].reshape(CH, KD))).astype(BF)

    done.append(copy(qsend, pq.at[core], p_s.at[1], p_r.at[1], partner))

    def spread(cc, n1, i1, peer1, n2, i2, peer2):
        w = n1 * QC
        blk = R * w
        sub = RQ * w
        sends = []

        def hops(n, b, d):
            return n // 2 if (b == 0) == (d == 0) else n - 1 - n // 2

        def ring(n, i, d, k):
            return lax.rem(i + (k if d == 0 else n - k), n)

        part_rows = CH // 2

        def cell(o2, o1, b):
            return rows(qall, (o2 * n1 + o1) * CH + b * part_rows, part_rows)

        def new_at(s):
            if s == 0:
                return [(b, i1, None) for b in range(2)]
            return [
                (b, ring(n1, i1, 1 - d, s), d)
                for b in range(2)
                for d in range(2)
                if s <= hops(n1, b, d)
            ]

        def first_copy(b, o1, d, h):
            _, dev = peer1(1 if d == 0 else n1 - 1)
            here = cell(i2, o1, b)
            return copy(here, here, a1_s.at[b, d, h], a1_r.at[b, o1], dev)

        def second_copy(b, o1, o2, d, h):
            _, dev = peer2(1 if d == 0 else n2 - 1)
            here = cell(o2, o1, b)
            return copy(here, here, a2_s.at[b, o1, d, h], a2_r.at[b, o1, o2], dev)

        def launch(c):
            c.start()
            sends.append(c)

        def gather_step(s):
            if s <= n1 // 2:
                for b, o1, d in new_at(s):
                    if s:
                        first_copy(b, o1, d, s).wait_recv()
                    for way in (0, 1) if d is None else (d,):
                        if s + 1 <= hops(n1, b, way):
                            launch(first_copy(b, o1, way, s + 1))
                    for way in range(2):
                        if hops(n2, b, way):
                            launch(second_copy(b, o1, i2, way, 1))
            for h in range(2, n2 // 2 + 1):
                if not 0 <= s - h + 1 <= n1 // 2:
                    continue
                for b, o1, _ in new_at(s - h + 1):
                    for way in range(2):
                        if h <= hops(n2, b, way):
                            o2 = ring(n2, i2, 1 - way, h - 1)
                            c = second_copy(b, o1, o2, way, h)
                            c.wait_recv()
                            launch(c)

        def settle(b):
            for k1 in range(n1):
                o1 = lax.rem(i1 + k1, n1)
                for k2 in range(1, n2):
                    o2 = lax.rem(i2 + k2, n2)
                    way = 1 if k2 <= hops(n2, b, 1) else 0
                    dist = k2 if way == 1 else n2 - k2
                    if dist == hops(n2, b, way):
                        second_copy(b, o1, o2, way, dist).wait_recv()

        if cc == 0:
            pq[0] = produce(0)
        else:
            to_partner(produce(0))
            incoming()
            pq[1] = produce(1)
        gather_chunk()
        qall[pl.ds(pl.multiple_of((i2 * n1 + i1) * CH, 16), CH), :] = ck[...]
        gather_step(0)
        if cc == 0:
            incoming()
            to_partner(produce(1))
        for s in range(1, n1 // 2 + max(1, n2 // 2)):
            gather_step(s)

        many = min(4, n1)
        span = many * QC
        mix = onehot(
            RB * span,
            RB * span,
            lambda i: i % span // QC * part_rows + i // span * QC + i % QC,
        ).astype(BF)

        def pack(b):
            def one(g, _):
                source = jnp.concatenate(
                    [
                        qall[
                            pl.ds(
                                pl.multiple_of((g * many + o) * CH + b * part_rows, 16), part_rows
                            ),
                            :,
                        ]
                        for o in range(many)
                    ],
                    0,
                )
                mixed = dot(mix, source).astype(BF)
                for r in range(RB):
                    here = pl.ds(pl.multiple_of(r * nq + g * span, 8), span)
                    qp[here, :] = mixed[r * span : (r + 1) * span]
                return 0

            lax.fori_loop(0, n1 * n2 // many, one, 0)

        nq = n2 * w
        big = n2 // 2
        copy(kx, ko, p_s.at[0], p_r.at[0], partner).wait_recv()
        if cc == 1:
            load_n.wait()

        st[...] = jnp.full(st.shape, NEG, F32)
        def attend(r, _):
            q = qp[pl.ds(pl.multiple_of(lax.rem(r, RB) * nq, 16), nq), :]
            if cc == 0:
                k_a, k_b = cvm[idx[r, 0]], ko[r]
            else:
                k_a, k_b = ko[r], nvm[r]
            mine = jnp.where(iota(lens_v.shape, 0) == r + cc * R, lens_v[...], 0)
            length = jnp.sum(mine, axis=0, keepdims=True)[:, :1]
            base = (shard - core) * seq
            place = base + lax.broadcasted_iota(jnp.int32, (nq, seq), 1)
            ok_a, ok_b = place < length, place + seq < length
            s_a = jnp.where(ok_a, dot(q, k_a) * scale, NEG)
            s_b = jnp.where(ok_b, dot(q, k_b) * scale, NEG)
            top = jnp.maximum(
                jnp.max(s_a, axis=1, keepdims=True), jnp.max(s_b, axis=1, keepdims=True)
            )
            p_a = jnp.where(ok_a, jnp.exp(s_a - top), 0.0)
            p_b = jnp.where(ok_b, jnp.exp(s_b - top), 0.0)
            total = jnp.sum(p_a, axis=1, keepdims=True) + jnp.sum(p_b, axis=1, keepdims=True)
            summed = dot_t(p_a.astype(BF), k_a[:DL, :]) + dot_t(p_b.astype(BF), k_b[:DL, :])
            some = total > 0.0
            safe = jnp.where(some, total, 1.0)
            value = (summed * (1.0 / safe)).astype(BF)
            lse = jnp.where(some, top + jnp.log(safe), NEG)
            for o in range(n2):
                acc[pl.ds(pl.multiple_of(o * blk + r * w, 16), w), :] = value[o * w : (o + 1) * w]
                column = jnp.where(iota((w, 128), 0) == iota((w, 128), 1), lse[o * w : (o + 1) * w], 0.0)
                line = jnp.sum(column, axis=0, keepdims=True)
                st[r // RQ, o] = jnp.where(iota((R, 128), 0) == r, line, st[r // RQ, o])
            return 0

        def slot(q, d, h):
            return q * (n2 - 1) + (0 if d == 0 else hops(n2, q % 2, 0)) + h - 1

        def merge(q, target, slots):
            parts = [st[q, target]] + [rss[s] for s in slots]
            top = functools.reduce(jnp.maximum, parts)
            weights = [jnp.exp(p - top) for p in parts]
            total = functools.reduce(jnp.add, weights)
            weights = [v / total for v in weights]
            st[q, target] = top + jnp.log(total)
            same = iota((w, 128), 0) == iota((w, 128), 1)
            for r in range(RQ):
                mine = pl.ds(pl.multiple_of(target * blk + q * sub + r * w, 16), w)
                values = [acc[mine, :]]
                for s in slots:
                    values.append(rsr[pl.ds(s * sub + r * w, w), :])
                out = None
                row = q * RQ + r
                for v, g in zip(values, weights):
                    col = jnp.sum(jnp.where(same, g[row : row + 1, :], 0.0), axis=1, keepdims=True)
                    term = v.astype(F32) * col
                    out = term if out is None else out + term
                acc[mine, :] = out.astype(BF)

        def reduce_copies(q, d, h, target, dev):
            s = slot(q, d, h)
            big_copy = copy(
                rows(acc, target * blk + q * sub, sub),
                rsr.at[pl.ds(s * sub, sub)],
                c_s.at[q, d, h],
                c_r.at[q, d, h],
                dev,
            )
            small_copy = copy(
                st.at[q, target], rss.at[s], d_s.at[q, d, h], d_r.at[q, d, h], dev
            )
            return big_copy, small_copy

        def step(q, d, h):
            if h > hops(n2, q % 2, d):
                return
            _, dev = peer2(1 if d == 0 else n2 - 1)
            target = ring(n2, i2, d, hops(n2, q % 2, d) - h + 1)
            if h > 1:
                for c in reduce_copies(q, d, h - 1, target, dev):
                    c.wait_recv()
                merge(q, target, [slot(q, d, h - 1)])
            for c in reduce_copies(q, d, h, target, dev):
                launch(c)

        for b in range(2):
            settle(b)
            pack(b)
            for q in (2 * b, 2 * b + 1):
                lax.fori_loop(q * RQ, (q + 1) * RQ, attend, 0)
                for d in range(2):
                    step(q, d, 1)
        for h in range(2, big + 1):
            for q in range(4):
                for d in range(2):
                    step(q, d, h)

        for b in range(2):
            for q in (2 * b, 2 * b + 1):
                slots = []
                for d in range(2):
                    last = hops(n2, q % 2, d)
                    if last:
                        _, dev = peer2(1 if d == 0 else n2 - 1)
                        for c in reduce_copies(q, d, last, i2, dev):
                            c.wait_recv()
                        slots.append(slot(q, d, last))
                if slots:
                    merge(q, i2, slots)
            block = pl.ds(pl.multiple_of(i2 * blk + 2 * b * sub, 16), 2 * sub)
            for k in range(1, n1 + 1):
                j, dev = peer1(k)
                sel = onehot(part_rows, 2 * sub, lambda i: i // QC * w + j * QC + i % QC)
                value = dot(sel.astype(BF), acc[block, :]).astype(BF)
                if k == n1:
                    rb[pl.ds(pl.multiple_of(i1 * CH + b * part_rows, 16), part_rows), :] = value
                    continue
                sb[k, b * part_rows : (b + 1) * part_rows] = value
                launch(
                    copy(
                        sb.at[k, pl.ds(b * part_rows, part_rows)],
                        rows(rb, i1 * CH + b * part_rows, part_rows),
                        e_s.at[k, b],
                        e_r.at[i1, b],
                        dev,
                    )
                )
        stats = st[0, i2]
        for q in range(1, 4):
            stats = jnp.where(iota((R, 128), 0) // RQ == q, st[q, i2], stats)
        for k in range(1, n1 + 1):
            j, dev = peer1(k)
            sel = onehot(128, 128, lambda i: jnp.where(i // QC == j, i % QC, -1))
            stat = dot(stats, sel, precision=lax.Precision.HIGHEST)
            if k == n1:
                rst[i1] = stat
                continue
            sst[k] = stat
            launch(copy(sst.at[k], rst.at[i1], f_s.at[k], f_r.at[i1], dev))
        for k in range(1, n1):
            j, dev = peer1(k)
            for b in range(2):
                copy(
                    sb.at[k, pl.ds(b * part_rows, part_rows)],
                    rows(rb, j * CH + b * part_rows, part_rows),
                    e_s.at[k, b],
                    e_r.at[j, b],
                    dev,
                ).wait_recv()
            copy(sst.at[k], rst.at[j], f_s.at[k], f_r.at[j], dev).wait_recv()

        if cc == 0:
            nkv = dot(sels[...], nkv_ref[...]).astype(BF)
        else:
            nkv = dot(fresh_rows(M)[1], yrecv[:, QB : QB + KD]).astype(BF)
        fresh = dot_t(ck[...], nkv) * scale
        i = lax.broadcasted_iota(jnp.int32, (CH, M), 0)
        j = lax.broadcasted_iota(jnp.int32, (CH, M), 1)
        seen = (i // QC == j // T) & (j % T <= i % QC // (2 * HL)) & (j < RT)
        fresh = jnp.where(seen, fresh, NEG)
        fill = onehot(CH, R, lambda i: i // QC)
        own_head = lax.broadcasted_iota(jnp.int32, (CH, 128), 0) % QC
        lane = lax.broadcasted_iota(jnp.int32, (CH, 128), 1)
        lses = []
        for s in range(n1):
            spread_out = dot(fill, rst[s], precision=lax.Precision.HIGHEST)
            lses.append(
                jnp.sum(jnp.where(lane == own_head, spread_out, 0.0), axis=1, keepdims=True)
            )
        top = functools.reduce(jnp.maximum, lses, jnp.max(fresh, axis=1, keepdims=True))
        probs = jnp.where(seen, jnp.exp(fresh - top), 0.0)
        total = jnp.sum(probs, axis=1, keepdims=True)
        summed = dot(probs.astype(BF), nkv[:, :DL])
        for s in range(n1):
            g = jnp.exp(lses[s] - top)
            total = total + g
            summed = summed + rb[s * CH : (s + 1) * CH, :].astype(F32) * g
        lat[...] = (summed / total).astype(BF)
        for c in sends:
            c.wait_send()

    @pl.when(core == 0)
    def _():
        spread(0, NX, x, x_peer, NZ, z, z_peer)

    @pl.when(core == 1)
    def _():
        spread(1, NZ, z, z_peer, NX, x, x_peer)

    def heads_of(cc):
        sel = onehot(
            HL * RT,
            CH,
            lambda i: i % RT // T * QC + i % T * (2 * HL) + cc * HL + i // RT,
        ).astype(BF)
        return dot(sel, lat[...]).astype(BF)

    fl[...] = heads_of(1 - core)
    swap = copy(fl, lo.at[core], p_s.at[2], p_r.at[2], partner)
    swap.start()
    done.append(swap)
    lo[core] = heads_of(core)
    copy(fl, lo.at[1 - core], p_s.at[2], p_r.at[2], partner).wait_recv()
    every = lo[...].reshape(2 * HL * RT, DL)
    flat = []
    for h in range(HL):
        value = dot(every, wuv_ref[h]).astype(BF)
        sel = onehot(M, 2 * HL * RT, lambda i: i // RT * (HL * RT) + h * RT + i % RT).astype(BF)
        flat.append(dot(sel, value).astype(BF))
    flat = jnp.concatenate(flat, 1)
    load_o.wait()
    group = 2 * NZL * NX
    swaps = []
    for g in range(NZ // NZL):
        span = slice(g * group * W, (g + 1) * group * W)
        part[:, span] = dot(flat, wov[:, span])
        for s in range(g * group, (g + 1) * group):
            s_pre, rest = divmod(s, 2 * NZL * NX)
            s_x, rest = divmod(rest, 2 * NZL)
            s_zl, s_core = divmod(rest, 2)
            first = s * W // 128
            off = s * W - first * 128
            if off + W <= 128:
                piece = part[:, first * 128 : (first + 1) * 128]
                if off:
                    piece = pltpu.roll(piece, 128 - off, 1)
            else:
                piece = pltpu.roll(part[:, first * 128 : (first + 2) * 128], 256 - off, 1)[:, :128]
            po[s_core, s_x, s_pre * NZL + s_zl] = piece
        zz = pl.ds(g * NZL, NZL)
        c = copy(po.at[1 - core, :, zz], pr.at[:, zz], w_s.at[g], w_r.at[g], partner)
        c.start()
        swaps.append(c)
        done.append(c)
    for c in swaps:
        c.wait_recv()
    po[core] = po[core] + pr[...]
    for k in range(1, NX):
        j, dev = x_peer(k)
        xs[k] = po[core, j].astype(BF)
        c = copy(xs.at[k], xr.at[x], x_s.at[k], x_r.at[x], dev)
        c.start()
        done.append(c)
    total = po[core, x]
    for k in range(1, NX):
        j, dev = x_peer(k)
        copy(xs.at[k], xr.at[j], x_s.at[k], x_r.at[j], dev).wait_recv()
        total = total + xr[j].astype(F32)
    zs[...] = total
    for k in range(1, NZ):
        j, dev = z_peer(k)
        c = copy(zs.at[j], zr.at[z], z_s.at[k], z_r.at[z], dev)
        c.start()
        done.append(c)
    total = zs[z]
    for k in range(1, NZ):
        j, dev = z_peer(k)
        copy(zs.at[j], zr.at[j], z_s.at[k], z_r.at[j], dev).wait_recv()
        total = total + zr[j]
    final = total.astype(BF)
    yos[...] = dot_c(pick[...], final).astype(BF)
    for k in range(1, G):
        gg, dev = g_peer(k)
        c = copy(rows(yos, gg * YP, YP), rows(yor, grp * YP, YP), o_s.at[k], o_r.at[grp], dev)
        c.start()
        done.append(c)
    yor[own, :] = yos[own, :]
    for k in range(1, G):
        gg, dev = g_peer(k)
        copy(
            rows(yos, gg * YP, YP), rows(yor, gg * YP, YP), o_s.at[k], o_r.at[gg], dev
        ).wait_recv()
    placed = dot_c(sels[...], final) + dot_c(sely[...], yor[...])
    out_ref[...] = placed[:, :W].astype(BF)
    for c in done:
        c.wait_send()


def local(sizes, cache, cache_len, new_latent, prompt_len, dest, q_latent, new_kv, w_uq, w_uk, w_uv, w_o):
    G, NX, NZ, NZL = sizes
    rows_n, seq, KD = cache.shape
    T, _, QL = q_latent.shape
    HL, DN, DL = w_uk.shape
    DR = KD - DL
    R = new_latent.shape[0]
    PERG = R // G
    YP = up(2 * PERG * T, 16)
    shards = 2 * NX * NZ
    W = w_o.shape[1] // shards
    M = 2 * R * T
    HM = up(R * T, 16)
    QC = T * 2 * HL
    CH = R * QC
    nq = NX * NZ * QC
    KP = up(KD, 128)
    QA = min(QL, up((QL + KP) // 2, 128))
    YW = max(QA, QL - QA + KP)
    half = DR // 2
    freq = ROPE_BASE ** (-jnp.arange(half, dtype=F32) / half)
    freq = jnp.concatenate([freq, freq])[None, :]
    dims = (G, NX, NZ, NZL, T, R, HL, PERG, YP, KD, DL, DN, DR, QL, W, rows_n, QA)
    tall = max(NX, NZ)

    def slots_rows(n1, n2, per):
        return 2 * (n2 - 1) * n1 * QC * per

    rsr_rows = max(slots_rows(NX, NZ, R // 2), slots_rows(NZ, NX, R // 2), 16)
    hop = tall // 2 + 1
    vmem = pl.BlockSpec(memory_space=pltpu.VMEM)
    anywhere = pl.BlockSpec(memory_space=pl.ANY)
    dma = pltpu.SemaphoreType.DMA
    V = pltpu.VMEM
    out = pl.pallas_call(
        functools.partial(kernel, dims),
        out_shape=jax.ShapeDtypeStruct((T * rows_n, W), BF),
        in_specs=[vmem] * 9 + [anywhere] * 3,
        out_specs=vmem,
        scratch_shapes=[
            V((rows_n, KD, seq), BF),
            V((R, KD, seq), BF),
            V(w_o.shape, BF),
            V((2 * R, 128), jnp.int32),
            pltpu.SMEM((2 * R, 128), jnp.int32),
            V((2 * R, 128), jnp.int32),
            V((M, T * rows_n), BF),
            V((G * YP, T * rows_n), BF),
            V((G * YP, T * rows_n), BF),
            V((M, G * YP), BF),
            V((T * rows_n, YW), BF),
            V((T * rows_n, YW), BF),
            V((G * YP, YW), BF),
            V((G * YP, YW), BF),
            V((R, KD, seq), BF),
            V((R, KD, seq), BF),
            V((HL, HM, KD), BF),
            V((HL * R * T, KD), BF),
            V((2, HL * R * T, KD), BF),
            V((CH, KD), BF),
            V((NX * NZ * CH, KD), BF),
            V((R // 2 * nq, KD), BF),
            V((R * nq, DL), BF),
            V((rsr_rows, DL), BF),
            V((4, tall, R, 128), F32),
            V((4 * (tall - 1), R, 128), F32),
            V((tall, CH, DL), BF),
            V((tall, R, 128), F32),
            V((tall * CH, DL), BF),
            V((tall, R, 128), F32),
            V((CH, DL), BF),
            V((2, HL * R * T, DL), BF),
            V((HL * R * T, DL), BF),
            V((M, shards * W), F32),
            V((2, NX, NZ, M, 128), F32),
            V((NX, NZ, M, 128), F32),
            V((NX, NZ, M, 128), BF),
            V((NX, NZ, M, 128), BF),
            V((NZ, M, 128), F32),
            V((NZ, M, 128), F32),
            V((G * YP, 128), BF),
            V((G * YP, 128), BF),
            dma((4,)), dma((G,)), dma((G,)), dma((4,)), dma((4,)),
            dma((2, 2, hop)), dma((2, tall)), dma((2, tall, 2, hop)), dma((2, tall, tall)),
            dma((4, 2, hop)), dma((4, 2, hop)), dma((4, 2, hop)), dma((4, 2, hop)),
            dma((tall, 2)), dma((tall, 2)), dma((tall,)), dma((tall,)),
            dma((NX,)), dma((NX,)), dma((NZ,)), dma((NZ,)), dma((G,)), dma((G,)),
            dma((NZ // NZL,)), dma((NZ // NZL,)),
        ],
        compiler_params=pltpu.CompilerParams(
            collective_id=0, has_side_effects=True, vmem_limit_bytes=60 * 2**20
        ),
    )(
        dest.T,
        cache_len[None, :],
        prompt_len[None, :],
        freq,
        q_latent.reshape(T * rows_n, QL),
        new_kv.reshape(T * rows_n, KD),
        w_uq,
        w_uk,
        w_uv,
        cache.transpose(0, 2, 1),
        new_latent.transpose(0, 2, 1),
        w_o,
    )
    return out.reshape(T, rows_n, W)


def solution(mesh):
    placed = (
        P("grp", ("pre", "dec"), None),
        P("grp"),
        P("grp", ("pre", "dec"), None),
        P(),
        P(),
        P(None, "grp", None),
        P(None, "grp", None),
        P(None, ("pre", "dec")),
        P(("pre", "dec"), None, None),
        P(("pre", "dec"), None, None),
        P(("pre", "dec"), None),
    )
    zl = 2
    sizes = (
        mesh.shape["grp"],
        mesh.shape["dec"] // (2 * zl),
        mesh.shape["pre"] * zl,
        zl,
    )
    return jax.shard_map(
        functools.partial(local, sizes),
        mesh=mesh,
        in_specs=placed,
        out_specs=P(None, "grp", ("pre", "dec")),
        check_vma=False,
    )
```

```python
import functools
import math

import jax
import jax.numpy as jnp
from jax import lax
from jax.experimental import pallas as pl
from jax.experimental.pallas import tpu as pltpu
from jax.sharding import PartitionSpec as P

ROPE_BASE = 10000.0
MESH = pl.DeviceIdType.MESH
NEG = -1e30
BF = jnp.bfloat16
F32 = jnp.float32


def up(value, unit):
    return -(-value // unit) * unit


def dot(a, b, **kw):
    return jnp.dot(a, b, preferred_element_type=F32, **kw)


def dot_t(a, b):
    return lax.dot_general(a, b, (((1,), (1,)), ((), ())), preferred_element_type=F32)


def dot_c(a, b):
    return lax.dot_general(a, b, (((0,), (0,)), ((), ())), preferred_element_type=F32)


def onehot(rows, cols, source):
    i = lax.broadcasted_iota(jnp.int32, (rows, cols), 0)
    j = lax.broadcasted_iota(jnp.int32, (rows, cols), 1)
    return jnp.where(source(i) == j, 1.0, 0.0)


def kernel(
    dims,
    dest_ref, clen_ref, plen_ref, freq_ref, ql_ref, nkv_ref, wuq_ref, wuk_ref, wuv_ref,
    cache_ref, newl_ref, wo_ref,
    out_ref,
    cvm, nvm, wov, idx_v, idx, lens_v, sels, sely, selh, pick, xlo, xhi,
    ysend, yrecv, kx, ko, qh, qsend, pq, ck, qall, qp, acc, rsr, st, rss,
    sb, sst, rb, rst, lat, lo, fl, part, po, pr, xs, xr, zs, zr, yos, yor,
    l_s, y_s, y_r, p_s, p_r, a1_s, a1_r, a2_s, a2_r, c_s, c_r, d_s, d_r,
    e_s, e_r, f_s, f_r, x_s, x_r, z_s, z_r, o_s, o_r, w_s, w_r,
):
    G, NX, NZ, NZL, T, R, HL, PERG, YP, KD, DL, DN, DR, QL, W, SLOTS, QA = dims
    QC = T * 2 * HL
    CH = R * QC
    RT = R * T
    M = 2 * RT
    HM = up(RT, 16)
    RB = R // 2
    RQ = R // 4
    QB = QL - QA
    NEW = G * R
    TS = T * SLOTS
    PT = PERG * T
    scale = 1.0 / math.sqrt(DN + DR)
    seq = cache_ref.shape[2]
    pre, grp, dec = lax.axis_index("pre"), lax.axis_index("grp"), lax.axis_index("dec")
    core = lax.rem(dec, 2)
    z = pre * NZL + lax.rem(dec // 2, NZL)
    x = dec // (2 * NZL)
    shard = pre * (2 * NZL * NX) + dec

    def at(xx, zz, cc, gg):
        return (zz // NZL, gg, xx * (2 * NZL) + lax.rem(zz, NZL) * 2 + cc)

    partner = at(x, z, 1 - core, grp)

    def x_peer(k):
        xx = lax.rem(x + k, NX)
        return xx, at(xx, z, core, grp)

    def z_peer(k):
        zz = lax.rem(z + k, NZ)
        return zz, at(x, zz, core, grp)

    def g_peer(k):
        gg = lax.rem(grp + k, G)
        return gg, at(x, z, core, gg)

    def copy(src, dst, s, r, dev):
        return pltpu.make_async_remote_copy(
            src_ref=src, dst_ref=dst, send_sem=s, recv_sem=r, device_id=dev, device_id_type=MESH
        )

    def rows(ref, start, count):
        return ref.at[pl.ds(pl.multiple_of(start, 16), count)]

    def iota(shape, axis):
        return lax.broadcasted_iota(jnp.int32, shape, axis)

    barrier = pltpu.get_barrier_semaphore()
    peers = [partner]
    peers += [x_peer(k)[1] for k in range(1, NX)]
    peers += [z_peer(k)[1] for k in range(1, NZ)]
    peers += [g_peer(k)[1] for k in range(1, G)]
    for dev in peers:
        pl.semaphore_signal(barrier, inc=1, device_id=dev, device_id_type=MESH)
    load_c = pltpu.make_async_copy(cache_ref, cvm, l_s.at[0])
    load_n = pltpu.make_async_copy(newl_ref, nvm, l_s.at[1])
    load_o = pltpu.make_async_copy(wo_ref, wov, l_s.at[2])
    load_c.start()

    to_row = dest_ref[0:1, :]
    spot_row = dest_ref[1:2, :]
    same = iota((NEW, NEW), 0) == iota((NEW, NEW), 1)
    to_col = jnp.sum(jnp.where(same, to_row, 0), axis=1, keepdims=True)
    spot_col = jnp.sum(jnp.where(same, spot_row, 0), axis=1, keepdims=True)
    here_row = to_row == grp
    hit = jnp.where((spot_row == iota((SLOTS, NEW), 0)) & here_row, 1, 0)
    left_col = 1 - jnp.sum(hit, axis=1, keepdims=True)

    def before(shape):
        slot = lax.rem(iota(shape, 1), SLOTS)
        return jnp.sum(jnp.where(iota(shape, 0) < slot, left_col, 0), axis=0, keepdims=True)

    def left(shape):
        slot = lax.rem(iota(shape, 1), SLOTS)
        return jnp.sum(jnp.where(iota(shape, 0) == slot, left_col, 0), axis=0, keepdims=True)

    before_t, left_t = before((SLOTS, TS)), left((SLOTS, TS))
    before_s, left_s = before((SLOTS, SLOTS)), left((SLOTS, SLOTS))
    is_surv = (before_s == iota((2 * R, SLOTS), 0)) & (left_s > 0) & (iota((2 * R, SLOTS), 0) < R)
    surv_col = jnp.sum(jnp.where(is_surv, iota((2 * R, SLOTS), 1), 0), axis=1, keepdims=True)
    idx_v[...] = jnp.broadcast_to(surv_col, idx_v.shape)
    fetch = pltpu.make_async_copy(idx_v, idx, l_s.at[3])
    fetch.start()
    row_of = iota((2 * R, NEW), 0) - R + grp * R
    is_mine = (iota((2 * R, NEW), 1) == row_of) & (iota((2 * R, NEW), 0) >= R)
    lens_col = jnp.sum(jnp.where(is_surv, clen_ref[...], 0), axis=1, keepdims=True) + jnp.sum(
        jnp.where(is_mine, plen_ref[...], 0), axis=1, keepdims=True
    )
    lens_v[...] = jnp.broadcast_to(lens_col, lens_v.shape)
    k_row, k_col = iota((NEW, NEW), 1), iota((NEW, NEW), 0)
    rank_row = jnp.sum(
        jnp.where((to_col == to_row) & (k_col // R == k_row // R) & (k_col < k_row), 1, 0),
        axis=0,
        keepdims=True,
    )
    i, j = iota((M, TS), 0), iota((M, TS), 1)
    sels[...] = jnp.where(
        (before_t == i // T) & (left_t > 0) & (j // SLOTS == i % T) & (i < RT), 1.0, 0.0
    ).astype(BF)
    i, j = iota((G * YP, NEW), 0), iota((G * YP, NEW), 1)
    u = i % YP
    from_k = jnp.where((j // R == i // YP) & here_row & (rank_row == u % PT // T), 1.0, 0.0)
    to_slot = jnp.where(spot_col == iota((NEW, TS), 1) % SLOTS, 1.0, 0.0)
    i, j = iota((G * YP, TS), 0), iota((G * YP, TS), 1)
    u = i % YP
    chosen = dot(from_k.astype(BF), to_slot.astype(BF))
    chosen = jnp.where(j // SLOTS == u % PT % T, chosen, 0.0)
    sely[...] = jnp.where(u < PT, chosen, 0.0).astype(BF)
    selh[...] = jnp.where((u >= PT) & (u < 2 * PT), chosen, 0.0).astype(BF)
    i, j = iota((M, NEW), 0), iota((M, NEW), 1)
    own_k = (j == (i - RT) // T + grp * R) & (i >= RT)
    key_col = jnp.sum(jnp.where(own_k, to_row * YP + rank_row * T, 0), axis=1, keepdims=True)
    i, j = iota((M, G * YP), 0), iota((M, G * YP), 1)
    pick[...] = jnp.where((key_col + i % T == j) & (i >= RT), 1.0, 0.0).astype(BF)
    xlo[...] = jnp.zeros(xlo.shape, BF)
    xhi[...] = jnp.zeros(xhi.shape, BF)
    xlo[:, :QA] = ql_ref[:, :QA]
    if QB:
        xhi[:, :QB] = ql_ref[:, QA:]
    xhi[:, QB : QB + KD] = nkv_ref[...]
    ysend[...] = (dot(sely[...], xlo[...]) + dot(selh[...], xhi[...])).astype(BF)
    half_dr = DR // 2
    lens_row = jnp.sum(
        jnp.where(iota((2 * R, 2 * R), 0) == iota((2 * R, 2 * R), 1), lens_col, 0),
        axis=0,
        keepdims=True,
    )

    def fresh_rows(count):
        i, j = iota((count, M), 0), iota((count, M), 1)
        low = jnp.where((j == i + RT) & (i < RT), 1.0, 0.0).astype(BF)
        low = dot(low, pick[...]).astype(BF)
        size = G * YP
        i, j = iota((size, size), 0), iota((size, size), 1)
        down = jnp.where(j == i + PT, 1.0, 0.0).astype(BF)
        return low, dot(low, down).astype(BF)

    def produce(half):
        i = iota((HM, 2 * R), 0)
        found = jnp.where((iota((HM, 2 * R), 1) == half * R + i // T) & (i < RT), lens_row, 0)
        pos = jnp.sum(found, axis=1, keepdims=True) + iota((HM, 1), 0) % T
        angle = pos.astype(F32) * freq_ref[...]
        cos, sin = jnp.cos(angle), jnp.sin(angle)
        sin = jnp.where(iota((HM, DR), 1) < half_dr, -sin, sin)
        if half == 0:
            xin = dot(sels[:HM, :], ql_ref[...]).astype(BF)
            qf = dot(xin, wuq_ref[...])
        else:
            low, high = fresh_rows(HM)
            qf = dot(dot(low, yrecv[:, :QA]).astype(BF), wuq_ref[:QA, :])
            if QB:
                qf = qf + dot(dot(high, yrecv[:, :QB]).astype(BF), wuq_ref[QA:, :])
        qf = qf.astype(BF)
        HD = DN + DR
        for h in range(HL):
            nope = dot(qf, onehot(HL * HD, DN, lambda i: i - h * HD).astype(BF)).astype(BF)
            qh[h, :, :DL] = dot(nope, wuk_ref[h]).astype(BF)
            turned = lambda i: jnp.where(
                (i >= h * HD + DN) & (i < (h + 1) * HD), (i - h * HD - DN + half_dr) % DR, -1
            )
            rot = dot(qf, onehot(HL * HD, DR, lambda i: i - h * HD - DN).astype(BF))
            swp = dot(qf, onehot(HL * HD, DR, turned).astype(BF))
            qh[h, :, DL:] = (rot * cos + swp * sin).astype(BF)
        total = None
        for h in range(HL):
            sel = onehot(
                HL * RT,
                HM,
                lambda i: jnp.where((i >= h * RT) & (i < (h + 1) * RT), i - h * RT, -1),
            ).astype(BF)
            term = dot(sel, qh[h])
            total = term if total is None else total + term
        return total.astype(BF)

    pl.semaphore_wait(barrier, len(peers))
    done = []
    for k in range(1, G):
        gg, dev = g_peer(k)
        c = copy(rows(ysend, gg * YP, YP), rows(yrecv, grp * YP, YP), y_s.at[k], y_r.at[grp], dev)
        c.start()
        done.append(c)
    own = pl.ds(pl.multiple_of(grp * YP, 16), YP)
    yrecv[own, :] = ysend[own, :]

    keys = copy(kx, ko, p_s.at[0], p_r.at[0], partner)
    done.append(keys)

    @pl.when(core == 0)
    def _():
        copy(newl_ref, ko, p_s.at[0], p_r.at[0], partner).start()

    fetch.wait()
    load_c.wait()

    @pl.when(core == 1)
    def _():
        for j in range(R):
            kx[j] = cvm[idx[j, 0]]
        keys.start()
        load_n.start()

    load_o.start()

    def incoming():
        for k in range(1, G):
            gg, dev = g_peer(k)
            copy(
                rows(ysend, gg * YP, YP), rows(yrecv, gg * YP, YP), y_s.at[k], y_r.at[gg], dev
            ).wait_recv()

    def to_partner(block):
        qsend[...] = block
        c = copy(qsend, pq.at[core], p_s.at[1], p_r.at[1], partner)
        c.start()

    def gather_chunk():
        copy(qsend, pq.at[1 - core], p_s.at[1], p_r.at[1], partner).wait_recv()
        regroup = onehot(
            CH, CH, lambda i: i % (2 * HL) * RT + i // QC * T + i % QC // (2 * HL)
        ).astype(BF)
        ck[...] = (dot(regroup, pq[...].reshape(CH, KD))).astype(BF)

    done.append(copy(qsend, pq.at[core], p_s.at[1], p_r.at[1], partner))

    def spread(cc, n1, i1, peer1, n2, i2, peer2):
        w = n1 * QC
        blk = R * w
        sub = RQ * w
        sends = []

        def hops(n, b, d):
            return n // 2 if (b == 0) == (d == 0) else n - 1 - n // 2

        def ring(n, i, d, k):
            return lax.rem(i + (k if d == 0 else n - k), n)

        part_rows = CH // 2

        def cell(o2, o1, b):
            return rows(qall, (o2 * n1 + o1) * CH + b * part_rows, part_rows)

        def new_at(s):
            if s == 0:
                return [(b, i1, None) for b in range(2)]
            return [
                (b, ring(n1, i1, 1 - d, s), d)
                for b in range(2)
                for d in range(2)
                if s <= hops(n1, b, d)
            ]

        def first_copy(b, o1, d, h):
            _, dev = peer1(1 if d == 0 else n1 - 1)
            here = cell(i2, o1, b)
            return copy(here, here, a1_s.at[b, d, h], a1_r.at[b, o1], dev)

        def second_copy(b, o1, o2, d, h):
            _, dev = peer2(1 if d == 0 else n2 - 1)
            here = cell(o2, o1, b)
            return copy(here, here, a2_s.at[b, o1, d, h], a2_r.at[b, o1, o2], dev)

        def launch(c):
            c.start()
            sends.append(c)

        def gather_step(s):
            if s <= n1 // 2:
                for b, o1, d in new_at(s):
                    if s:
                        first_copy(b, o1, d, s).wait_recv()
                    for way in (0, 1) if d is None else (d,):
                        if s + 1 <= hops(n1, b, way):
                            launch(first_copy(b, o1, way, s + 1))
                    for way in range(2):
                        if hops(n2, b, way):
                            launch(second_copy(b, o1, i2, way, 1))
            for h in range(2, n2 // 2 + 1):
                if not 0 <= s - h + 1 <= n1 // 2:
                    continue
                for b, o1, _ in new_at(s - h + 1):
                    for way in range(2):
                        if h <= hops(n2, b, way):
                            o2 = ring(n2, i2, 1 - way, h - 1)
                            c = second_copy(b, o1, o2, way, h)
                            c.wait_recv()
                            launch(c)

        def settle(b):
            for k1 in range(n1):
                o1 = lax.rem(i1 + k1, n1)
                for k2 in range(1, n2):
                    o2 = lax.rem(i2 + k2, n2)
                    way = 1 if k2 <= hops(n2, b, 1) else 0
                    dist = k2 if way == 1 else n2 - k2
                    if dist == hops(n2, b, way):
                        second_copy(b, o1, o2, way, dist).wait_recv()

        if cc == 0:
            pq[0] = produce(0)
        else:
            to_partner(produce(0))
            incoming()
            pq[1] = produce(1)
        gather_chunk()
        qall[pl.ds(pl.multiple_of((i2 * n1 + i1) * CH, 16), CH), :] = ck[...]
        gather_step(0)
        if cc == 0:
            incoming()
            to_partner(produce(1))
        for s in range(1, n1 // 2 + max(1, n2 // 2)):
            gather_step(s)

        many = min(4, n1)
        span = many * QC
        mix = onehot(
            RB * span,
            RB * span,
            lambda i: i % span // QC * part_rows + i // span * QC + i % QC,
        ).astype(BF)

        def pack(b):
            def one(g, _):
                source = jnp.concatenate(
                    [
                        qall[
                            pl.ds(
                                pl.multiple_of((g * many + o) * CH + b * part_rows, 16), part_rows
                            ),
                            :,
                        ]
                        for o in range(many)
                    ],
                    0,
                )
                mixed = dot(mix, source).astype(BF)
                for r in range(RB):
                    here = pl.ds(pl.multiple_of(r * nq + g * span, 8), span)
                    qp[here, :] = mixed[r * span : (r + 1) * span]
                return 0

            lax.fori_loop(0, n1 * n2 // many, one, 0)

        nq = n2 * w
        big = n2 // 2
        copy(kx, ko, p_s.at[0], p_r.at[0], partner).wait_recv()
        if cc == 1:
            load_n.wait()

        st[...] = jnp.full(st.shape, NEG, F32)
        def attend(r, _):
            q = qp[pl.ds(pl.multiple_of(lax.rem(r, RB) * nq, 16), nq), :]
            if cc == 0:
                k_a, k_b = cvm[idx[r, 0]], ko[r]
            else:
                k_a, k_b = ko[r], nvm[r]
            mine = jnp.where(iota(lens_v.shape, 0) == r + cc * R, lens_v[...], 0)
            length = jnp.sum(mine, axis=0, keepdims=True)[:, :1]
            base = (shard - core) * seq
            place = base + lax.broadcasted_iota(jnp.int32, (nq, seq), 1)
            ok_a, ok_b = place < length, place + seq < length
            s_a = jnp.where(ok_a, dot(q, k_a) * scale, NEG)
            s_b = jnp.where(ok_b, dot(q, k_b) * scale, NEG)
            top = jnp.maximum(
                jnp.max(s_a, axis=1, keepdims=True), jnp.max(s_b, axis=1, keepdims=True)
            )
            p_a = jnp.where(ok_a, jnp.exp(s_a - top), 0.0)
            p_b = jnp.where(ok_b, jnp.exp(s_b - top), 0.0)
            total = jnp.sum(p_a, axis=1, keepdims=True) + jnp.sum(p_b, axis=1, keepdims=True)
            summed = dot_t(p_a.astype(BF), k_a[:DL, :]) + dot_t(p_b.astype(BF), k_b[:DL, :])
            some = total > 0.0
            safe = jnp.where(some, total, 1.0)
            value = (summed * (1.0 / safe)).astype(BF)
            lse = jnp.where(some, top + jnp.log(safe), NEG)
            for o in range(n2):
                acc[pl.ds(pl.multiple_of(o * blk + r * w, 16), w), :] = value[o * w : (o + 1) * w]
                column = jnp.where(iota((w, 128), 0) == iota((w, 128), 1), lse[o * w : (o + 1) * w], 0.0)
                line = jnp.sum(column, axis=0, keepdims=True)
                st[r // RQ, o] = jnp.where(iota((R, 128), 0) == r, line, st[r // RQ, o])
            return 0

        def slot(q, d, h):
            return q * (n2 - 1) + (0 if d == 0 else hops(n2, q % 2, 0)) + h - 1

        def merge(q, target, slots):
            parts = [st[q, target]] + [rss[s] for s in slots]
            top = functools.reduce(jnp.maximum, parts)
            weights = [jnp.exp(p - top) for p in parts]
            total = functools.reduce(jnp.add, weights)
            weights = [v / total for v in weights]
            st[q, target] = top + jnp.log(total)
            same = iota((w, 128), 0) == iota((w, 128), 1)
            for r in range(RQ):
                mine = pl.ds(pl.multiple_of(target * blk + q * sub + r * w, 16), w)
                values = [acc[mine, :]]
                for s in slots:
                    values.append(rsr[pl.ds(s * sub + r * w, w), :])
                out = None
                row = q * RQ + r
                for v, g in zip(values, weights):
                    col = jnp.sum(jnp.where(same, g[row : row + 1, :], 0.0), axis=1, keepdims=True)
                    term = v.astype(F32) * col
                    out = term if out is None else out + term
                acc[mine, :] = out.astype(BF)

        def reduce_copies(q, d, h, target, dev):
            s = slot(q, d, h)
            big_copy = copy(
                rows(acc, target * blk + q * sub, sub),
                rsr.at[pl.ds(s * sub, sub)],
                c_s.at[q, d, h],
                c_r.at[q, d, h],
                dev,
            )
            small_copy = copy(
                st.at[q, target], rss.at[s], d_s.at[q, d, h], d_r.at[q, d, h], dev
            )
            return big_copy, small_copy

        def step(q, d, h):
            if h > hops(n2, q % 2, d):
                return
            _, dev = peer2(1 if d == 0 else n2 - 1)
            target = ring(n2, i2, d, hops(n2, q % 2, d) - h + 1)
            if h > 1:
                for c in reduce_copies(q, d, h - 1, target, dev):
                    c.wait_recv()
                merge(q, target, [slot(q, d, h - 1)])
            for c in reduce_copies(q, d, h, target, dev):
                launch(c)

        for b in range(2):
            settle(b)
            pack(b)
            for q in (2 * b, 2 * b + 1):
                lax.fori_loop(q * RQ, (q + 1) * RQ, attend, 0)
                for d in range(2):
                    step(q, d, 1)
        for h in range(2, big + 1):
            for q in range(4):
                for d in range(2):
                    step(q, d, h)

        def line_slot(b, d, h):
            return b * (n1 - 1) + (0 if d == 0 else hops(n1, b, 0)) + h - 1

        def line_copies(b, d, h, k):
            _, dev = peer1(1 if d == 0 else n1 - 1)
            s = line_slot(b, d, h)
            return (
                copy(sb.at[k, b], rb.at[s], e_s.at[b, d, h], e_r.at[b, d, h], dev),
                copy(sst.at[k, b], rst.at[s], f_s.at[b, d, h], f_r.at[b, d, h], dev),
            )

        def columns(b, g):
            fill = onehot(part_rows, R, lambda i: b * RB + i // QC)
            wide = dot(fill, g, precision=lax.Precision.HIGHEST)
            head = iota((part_rows, 128), 0) % QC
            return jnp.sum(
                jnp.where(iota((part_rows, 128), 1) == head, wide, 0.0), axis=1, keepdims=True
            )

        def line_step(b, d, h):
            if h > hops(n1, b, d):
                return
            ahead = hops(n1, b, d) - h + 1
            k = ahead if d == 0 else n1 - ahead
            if h > 1:
                for c in line_copies(b, d, h - 1, k):
                    c.wait_recv()
                s = line_slot(b, d, h - 1)
                own, came = sst[k, b], rst[s]
                top = jnp.maximum(own, came)
                g_own, g_came = jnp.exp(own - top), jnp.exp(came - top)
                total = g_own + g_came
                sst[k, b] = top + jnp.log(total)
                summed = sb[k, b].astype(F32) * columns(b, g_own / total)
                summed = summed + rb[s].astype(F32) * columns(b, g_came / total)
                sb[k, b] = summed.astype(BF)
            for c in line_copies(b, d, h, k):
                launch(c)

        for b in range(2):
            for q in (2 * b, 2 * b + 1):
                slots = []
                for d in range(2):
                    last = hops(n2, q % 2, d)
                    if last:
                        _, dev = peer2(1 if d == 0 else n2 - 1)
                        for c in reduce_copies(q, d, last, i2, dev):
                            c.wait_recv()
                        slots.append(slot(q, d, last))
                if slots:
                    merge(q, i2, slots)
            block = pl.ds(pl.multiple_of(i2 * blk + 2 * b * sub, 16), 2 * sub)
            stats = jnp.where(iota((R, 128), 0) // RQ == 2 * b, st[2 * b, i2], st[2 * b + 1, i2])
            for k in range(1, n1 + 1):
                j, dev = peer1(k)
                sel = onehot(part_rows, 2 * sub, lambda i: i // QC * w + j * QC + i % QC)
                sb[k % n1, b] = dot(sel.astype(BF), acc[block, :]).astype(BF)
                sel = onehot(128, 128, lambda i: jnp.where(i // QC == j, i % QC, -1))
                sst[k % n1, b] = dot(stats, sel, precision=lax.Precision.HIGHEST)
            for d in range(2):
                line_step(b, d, 1)
        for h in range(2, n1 // 2 + 1):
            for b in range(2):
                for d in range(2):
                    line_step(b, d, h)

        if cc == 0:
            nkv = dot(sels[...], nkv_ref[...]).astype(BF)
        else:
            nkv = dot(fresh_rows(M)[1], yrecv[:, QB : QB + KD]).astype(BF)
        fresh = dot_t(ck[...], nkv) * scale
        i = lax.broadcasted_iota(jnp.int32, (CH, M), 0)
        j = lax.broadcasted_iota(jnp.int32, (CH, M), 1)
        seen = (i // QC == j // T) & (j % T <= i % QC // (2 * HL)) & (j < RT)
        fresh = jnp.where(seen, fresh, NEG)
        parts = [([sb[0, b] for b in range(2)], [columns(b, sst[0, b]) for b in range(2)])]
        for d in range(2):
            values, stats = [], []
            for b in range(2):
                last = hops(n1, b, d)
                if last:
                    for c in line_copies(b, d, last, 0):
                        c.wait_recv()
                    s = line_slot(b, d, last)
                    values.append(rb[s])
                    stats.append(columns(b, rst[s]))
                else:
                    values.append(jnp.zeros((part_rows, DL), BF))
                    stats.append(jnp.full((part_rows, 1), NEG, F32))
            parts.append((values, stats))
        lses = [jnp.concatenate(stats, 0) for _, stats in parts]
        top = functools.reduce(jnp.maximum, lses, jnp.max(fresh, axis=1, keepdims=True))
        probs = jnp.where(seen, jnp.exp(fresh - top), 0.0)
        total = jnp.sum(probs, axis=1, keepdims=True)
        summed = dot(probs.astype(BF), nkv[:, :DL])
        for (values, _), lse in zip(parts, lses):
            g = jnp.exp(lse - top)
            total = total + g
            summed = summed + jnp.concatenate(values, 0).astype(F32) * g
        lat[...] = (summed / total).astype(BF)
        for c in sends:
            c.wait_send()

    @pl.when(core == 0)
    def _():
        spread(0, NX, x, x_peer, NZ, z, z_peer)

    @pl.when(core == 1)
    def _():
        spread(1, NZ, z, z_peer, NX, x, x_peer)

    def heads_of(cc):
        sel = onehot(
            HL * RT,
            CH,
            lambda i: i % RT // T * QC + i % T * (2 * HL) + cc * HL + i // RT,
        ).astype(BF)
        return dot(sel, lat[...]).astype(BF)

    fl[...] = heads_of(1 - core)
    swap = copy(fl, lo.at[core], p_s.at[2], p_r.at[2], partner)
    swap.start()
    done.append(swap)
    lo[core] = heads_of(core)
    copy(fl, lo.at[1 - core], p_s.at[2], p_r.at[2], partner).wait_recv()
    every = lo[...].reshape(2 * HL * RT, DL)
    flat = []
    for h in range(HL):
        value = dot(every, wuv_ref[h]).astype(BF)
        sel = onehot(M, 2 * HL * RT, lambda i: i // RT * (HL * RT) + h * RT + i % RT).astype(BF)
        flat.append(dot(sel, value).astype(BF))
    flat = jnp.concatenate(flat, 1)
    load_o.wait()
    group = 2 * NZL * NX
    swaps = []
    for g in range(NZ // NZL):
        span = slice(g * group * W, (g + 1) * group * W)
        part[:, span] = dot(flat, wov[:, span])
        for s in range(g * group, (g + 1) * group):
            s_pre, rest = divmod(s, 2 * NZL * NX)
            s_x, rest = divmod(rest, 2 * NZL)
            s_zl, s_core = divmod(rest, 2)
            first = s * W // 128
            off = s * W - first * 128
            if off + W <= 128:
                piece = part[:, first * 128 : (first + 1) * 128]
                if off:
                    piece = pltpu.roll(piece, 128 - off, 1)
            else:
                piece = pltpu.roll(part[:, first * 128 : (first + 2) * 128], 256 - off, 1)[:, :128]
            po[s_core, s_x, s_pre * NZL + s_zl] = piece
        zz = pl.ds(g * NZL, NZL)
        c = copy(po.at[1 - core, :, zz], pr.at[:, zz], w_s.at[g], w_r.at[g], partner)
        c.start()
        swaps.append(c)
        done.append(c)
    for c in swaps:
        c.wait_recv()
    po[core] = po[core] + pr[...]
    for k in range(1, NX):
        j, dev = x_peer(k)
        xs[k] = po[core, j].astype(BF)
        c = copy(xs.at[k], xr.at[x], x_s.at[k], x_r.at[x], dev)
        c.start()
        done.append(c)
    total = po[core, x]
    for k in range(1, NX):
        j, dev = x_peer(k)
        copy(xs.at[k], xr.at[j], x_s.at[k], x_r.at[j], dev).wait_recv()
        total = total + xr[j].astype(F32)
    zs[...] = total
    for k in range(1, NZ):
        j, dev = z_peer(k)
        c = copy(zs.at[j], zr.at[z], z_s.at[k], z_r.at[z], dev)
        c.start()
        done.append(c)
    total = zs[z]
    for k in range(1, NZ):
        j, dev = z_peer(k)
        copy(zs.at[j], zr.at[j], z_s.at[k], z_r.at[j], dev).wait_recv()
        total = total + zr[j]
    final = total.astype(BF)
    yos[...] = dot_c(pick[...], final).astype(BF)
    for k in range(1, G):
        gg, dev = g_peer(k)
        c = copy(rows(yos, gg * YP, YP), rows(yor, grp * YP, YP), o_s.at[k], o_r.at[grp], dev)
        c.start()
        done.append(c)
    yor[own, :] = yos[own, :]
    for k in range(1, G):
        gg, dev = g_peer(k)
        copy(
            rows(yos, gg * YP, YP), rows(yor, gg * YP, YP), o_s.at[k], o_r.at[gg], dev
        ).wait_recv()
    placed = dot_c(sels[...], final) + dot_c(sely[...], yor[...])
    out_ref[...] = placed[:, :W].astype(BF)
    for c in done:
        c.wait_send()


def local(sizes, cache, cache_len, new_latent, prompt_len, dest, q_latent, new_kv, w_uq, w_uk, w_uv, w_o):
    G, NX, NZ, NZL = sizes
    rows_n, seq, KD = cache.shape
    T, _, QL = q_latent.shape
    HL, DN, DL = w_uk.shape
    DR = KD - DL
    R = new_latent.shape[0]
    PERG = R // G
    YP = up(2 * PERG * T, 16)
    shards = 2 * NX * NZ
    W = w_o.shape[1] // shards
    M = 2 * R * T
    HM = up(R * T, 16)
    QC = T * 2 * HL
    CH = R * QC
    nq = NX * NZ * QC
    KP = up(KD, 128)
    QA = min(QL, up((QL + KP) // 2, 128))
    YW = max(QA, QL - QA + KP)
    half = DR // 2
    freq = ROPE_BASE ** (-jnp.arange(half, dtype=F32) / half)
    freq = jnp.concatenate([freq, freq])[None, :]
    dims = (G, NX, NZ, NZL, T, R, HL, PERG, YP, KD, DL, DN, DR, QL, W, rows_n, QA)
    tall = max(NX, NZ)

    def slots_rows(n1, n2, per):
        return 2 * (n2 - 1) * n1 * QC * per

    rsr_rows = max(slots_rows(NX, NZ, R // 2), slots_rows(NZ, NX, R // 2), 16)
    hop = tall // 2 + 1
    vmem = pl.BlockSpec(memory_space=pltpu.VMEM)
    anywhere = pl.BlockSpec(memory_space=pl.ANY)
    dma = pltpu.SemaphoreType.DMA
    V = pltpu.VMEM
    out = pl.pallas_call(
        functools.partial(kernel, dims),
        out_shape=jax.ShapeDtypeStruct((T * rows_n, W), BF),
        in_specs=[vmem] * 9 + [anywhere] * 3,
        out_specs=vmem,
        scratch_shapes=[
            V((rows_n, KD, seq), BF),
            V((R, KD, seq), BF),
            V(w_o.shape, BF),
            V((2 * R, 128), jnp.int32),
            pltpu.SMEM((2 * R, 128), jnp.int32),
            V((2 * R, 128), jnp.int32),
            V((M, T * rows_n), BF),
            V((G * YP, T * rows_n), BF),
            V((G * YP, T * rows_n), BF),
            V((M, G * YP), BF),
            V((T * rows_n, YW), BF),
            V((T * rows_n, YW), BF),
            V((G * YP, YW), BF),
            V((G * YP, YW), BF),
            V((R, KD, seq), BF),
            V((R, KD, seq), BF),
            V((HL, HM, KD), BF),
            V((HL * R * T, KD), BF),
            V((2, HL * R * T, KD), BF),
            V((CH, KD), BF),
            V((NX * NZ * CH, KD), BF),
            V((R // 2 * nq, KD), BF),
            V((R * nq, DL), BF),
            V((rsr_rows, DL), BF),
            V((4, tall, R, 128), F32),
            V((4 * (tall - 1), R, 128), F32),
            V((tall, 2, CH // 2, DL), BF),
            V((tall, 2, R, 128), F32),
            V((2 * (tall - 1), CH // 2, DL), BF),
            V((2 * (tall - 1), R, 128), F32),
            V((CH, DL), BF),
            V((2, HL * R * T, DL), BF),
            V((HL * R * T, DL), BF),
            V((M, shards * W), F32),
            V((2, NX, NZ, M, 128), F32),
            V((NX, NZ, M, 128), F32),
            V((NX, NZ, M, 128), BF),
            V((NX, NZ, M, 128), BF),
            V((NZ, M, 128), F32),
            V((NZ, M, 128), F32),
            V((G * YP, 128), BF),
            V((G * YP, 128), BF),
            dma((4,)), dma((G,)), dma((G,)), dma((4,)), dma((4,)),
            dma((2, 2, hop)), dma((2, tall)), dma((2, tall, 2, hop)), dma((2, tall, tall)),
            dma((4, 2, hop)), dma((4, 2, hop)), dma((4, 2, hop)), dma((4, 2, hop)),
            dma((2, 2, hop)), dma((2, 2, hop)), dma((2, 2, hop)), dma((2, 2, hop)),
            dma((NX,)), dma((NX,)), dma((NZ,)), dma((NZ,)), dma((G,)), dma((G,)),
            dma((NZ // NZL,)), dma((NZ // NZL,)),
        ],
        compiler_params=pltpu.CompilerParams(
            collective_id=0, has_side_effects=True, vmem_limit_bytes=60 * 2**20
        ),
    )(
        dest.T,
        cache_len[None, :],
        prompt_len[None, :],
        freq,
        q_latent.reshape(T * rows_n, QL),
        new_kv.reshape(T * rows_n, KD),
        w_uq,
        w_uk,
        w_uv,
        cache.transpose(0, 2, 1),
        new_latent.transpose(0, 2, 1),
        w_o,
    )
    return out.reshape(T, rows_n, W)


def solution(mesh):
    placed = (
        P("grp", ("pre", "dec"), None),
        P("grp"),
        P("grp", ("pre", "dec"), None),
        P(),
        P(),
        P(None, "grp", None),
        P(None, "grp", None),
        P(None, ("pre", "dec")),
        P(("pre", "dec"), None, None),
        P(("pre", "dec"), None, None),
        P(("pre", "dec"), None),
    )
    zl = 2
    sizes = (
        mesh.shape["grp"],
        mesh.shape["dec"] // (2 * zl),
        mesh.shape["pre"] * zl,
        zl,
    )
    return jax.shard_map(
        functools.partial(local, sizes),
        mesh=mesh,
        in_specs=placed,
        out_specs=P(None, "grp", ("pre", "dec")),
        check_vma=False,
    )
```
